256 devices in a mesh: grp: 4 (over y), dev: 64 (over x, z, core).
Axes of the slice: x: 4, y: 4, z: 8, core: 2. Of those that a mesh axis runs over, the one named last changes fastest.
Arguments:
- x_rows: bfloat16 [32768, 8192], P(('grp', 'dev')), may hold values from -6 to 6
- dt_rows: bfloat16 [32768, 128], P(('grp', 'dev')), may hold values from 0.0004 to 0.56
- bc_rows: bfloat16 [32768, 256], P(('grp', 'dev')), may hold values from -2 to 2
- a_log: float32 [128], P('dev'), may hold values from -0.35 to 0.35
- d_skip: float32 [128], P('dev'), may hold values from 0.5 to 1.5
- state_pool: float32 [64, 128, 64, 128], P('grp', 'dev'), may hold values from -2 to 2
- owners: int32 [128], P('grp'), may hold values from 0 to 63
- queries: bfloat16 [32768, 4096], P(('grp', 'dev')), may hold values from -6 to 6
- new_kv: bfloat16 [32768, 2048], P(('grp', 'dev')), may hold values from -6 to 6
- page_pool: bfloat16 [2048, 16, 2048], P(('grp', 'dev')), may hold values from -6 to 6
- page_table: int32 [128, 64], P('grp'), may hold values from 0 to 511, as said below
- prefix_len: int32 [128], P('grp'), may hold values from 256 to 1024, as said below
Outputs:
- ssd_out: bfloat16 [32768, 8192], P('grp', 'dev')
- final_states: float32 [128, 128, 64, 128], P('grp', 'dev')
- attn_out: bfloat16 [32768, 4096], P(('grp', 'dev'))
The draws below stay inside these ranges and needn't reach their ends.
Inputs may be any that keep to these rules, and one draw needn't show every extreme that they name: `page_table`: id // 8 is the index along dev of the device of the request's group that holds the page, id % 8 its place there; each row holds exactly 1 ids of every such device. `prefix_len`: the largest equals 1024.
All inputs are finite; a program needn't handle non-finite values.
Results may differ from the reference program's by a relative error of at most 0.0045.
Values may be sent and summed in bfloat16 or wider, within the bound.
A program may use at most 128 MiB of HBM per device.

```python
import math
import jax
import jax.numpy as jnp
from jax import lax

MIXER_HEADS = 128
P_SIZE = 64
N = 128
QH = 32
KVH = 8
HD = 128
NEW = 256
PAGE = 16
PREFIX = 1024
REQ = 32
REQS = 128
TOKEN_TOTAL = 32768
PPR = 64
PG_DEV = 8
PAGES = 2048
SLOTS = 64
N_GRP = 4
N_DEV = 64


def draw_queries(key, part):
    key = jax.random.fold_in(key, 31)
    key_values = jax.random.fold_in(key, 0)
    values = jnp.clip(jax.random.normal(key_values, (TOKEN_TOTAL, QH * HD), jnp.float32), -6.0, 6.0)
    return values.astype(jnp.bfloat16)


def draw_new_kv(key, part):
    key = jax.random.fold_in(key, 37)
    values = jnp.clip(jax.random.normal(key, (TOKEN_TOTAL, 2 * KVH * HD), jnp.float32), -6.0, 6.0)
    return values.astype(jnp.bfloat16)


def draw_dt_rows(key, part):
    key = jax.random.fold_in(key, 21)
    random_splits = jax.random.split(key, 4)
    lowest, highest = (0.002, 0.04)
    baseline_arrival_rate = jnp.exp(jax.random.uniform(random_splits[0], (MIXER_HEADS,), jnp.float32, math.log(lowest), math.log(highest)))
    jitter_level = jax.random.uniform(random_splits[1], (TOKEN_TOTAL, MIXER_HEADS), jnp.float32, 0.5, 1.5)
    arrival_spikes = (jax.random.uniform(random_splits[2], (TOKEN_TOTAL, MIXER_HEADS), jnp.float32) < 1.0 / 64.0).astype(jnp.float32)
    spike_length = jax.random.uniform(random_splits[3], (TOKEN_TOTAL, MIXER_HEADS), jnp.float32, 0.3, 0.5)
    return (baseline_arrival_rate[None, :] * jitter_level + arrival_spikes * spike_length).astype(jnp.bfloat16)


def draw_page_table(key, part):
    key = jax.random.fold_in(key, 11)
    random_splits = jax.random.split(key, 5)
    families = 4 * N_GRP
    family_id = jnp.arange(REQS, dtype=jnp.int32) // REQ * 4 + jax.random.randint(random_splits[0], (REQS,), 0, 4)
    orders = jax.vmap(lambda one_key: jax.random.permutation(one_key, PPR))(jax.random.split(random_splits[1], families))
    holders = (orders % N_DEV).astype(jnp.int32)
    family_slots = jax.random.randint(random_splits[2], (families, PPR), 0, PG_DEV)
    own_slots = jax.random.randint(random_splits[3], (REQS, PPR), 0, PG_DEV)
    shared_len = jax.random.randint(random_splits[4], (REQS,), 0, PPR + 1)
    column = jnp.arange(PPR, dtype=jnp.int32)
    slot_ids = jnp.where(column[None, :] < shared_len[:, None], family_slots[family_id], own_slots)
    return (holders[family_id] * PG_DEV + slot_ids).astype(jnp.int32)


def draw_prefix_len(key, part):
    key = jax.random.fold_in(key, 13)
    key_lengths, key_longest = jax.random.split(key)
    lengths = jax.random.randint(key_lengths, (REQS,), PREFIX // 4, PREFIX + 1)
    longest = jax.random.randint(key_longest, (), 0, REQS)
    return lengths.at[longest].set(PREFIX).astype(jnp.int32)


def with_ends(entries, key, low, high):
    dims = entries.shape
    place = [jax.random.randint(jax.random.fold_in(key, axis), (), 0, dims[axis]) for axis in range(len(dims))]
    entries = entries.at[tuple(place)].set(low)
    longest = dims.index(max(dims))
    place[longest] = (place[longest] + 1) % dims[longest]
    return entries.at[tuple(place)].set(high)


def level_of(own_key, dims, shards, low, largest):
    gain = 1.0
    for axis_at, blocks in shards:
        steps = jax.random.uniform(jax.random.fold_in(jax.random.fold_in(own_key, 6), axis_at), (blocks,), jnp.float32, low / len(shards), largest / len(shards))
        gain = gain * jnp.repeat(jnp.exp(steps), dims[axis_at] // blocks).reshape((-1,) + (1,) * (len(dims) - 1 - axis_at))
    return gain


def gaussian(key, extent, deviation, bound, cuts=(), kind=jnp.bfloat16):
    loudness = level_of(key, extent, cuts, -0.22, 0.18) if cuts else 1.0
    result = jax.random.normal(key, extent, jnp.float32) * deviation * loudness
    return jnp.minimum(jnp.maximum(result, -bound), bound).astype(kind)


def setup_inputs(seed: int = 0) -> dict:
    splits = jax.random.split(jax.random.key(seed), 13)
    return {
        "x_rows": gaussian(splits[0], (TOKEN_TOTAL, MIXER_HEADS * P_SIZE), 1.0, 6.0, ((0, 256),)),
        "dt_rows": draw_dt_rows(jax.random.fold_in(splits[12], 71), 0),
        "bc_rows": gaussian(splits[2], (TOKEN_TOTAL, 2 * N), 0.3, 2.0, ((0, 256),)),
        "a_log": jnp.clip(jax.random.uniform(splits[3], (MIXER_HEADS,), jnp.float32, -0.35, 0.35) * level_of(splits[3], (MIXER_HEADS,), ((0, 64),), -0.4, 0.0), -0.35, 0.35),
        "d_skip": jnp.clip(0.5 + 1.0 * jax.random.uniform(splits[4], (MIXER_HEADS,), jnp.float32) ** level_of(splits[4], (MIXER_HEADS,), ((0, 64),), -0.2, 0.2), 0.5, 1.5),
        "state_pool": gaussian(splits[5], (SLOTS, MIXER_HEADS, P_SIZE, N), 0.3, 2.0, ((0, 4), (1, 64)), jnp.float32),
        "owners": with_ends(jax.random.randint(splits[6], (REQS,), 0, SLOTS), jax.random.fold_in(splits[6], 1), 0, SLOTS - 1).astype(jnp.int32),
        "queries": draw_queries(jax.random.fold_in(splits[12], 71), 0),
        "new_kv": draw_new_kv(jax.random.fold_in(splits[12], 71), 0),
        "page_pool": gaussian(splits[9], (PAGES, PAGE, 2 * KVH * HD), 1.0, 6.0, ((0, 256),)),
        "page_table": draw_page_table(jax.random.fold_in(splits[12], 71), 0),
        "prefix_len": draw_prefix_len(jax.random.fold_in(splits[12], 71), 0),
    }


def attend(q_rows, key_rows, visible, kv_heads, head_size):
    row_count = q_rows.shape[0]
    groups = q_rows.shape[1] // (kv_heads * head_size)
    score_scale = 1.0 / math.sqrt(head_size)
    outputs = []
    for kv_head in range(kv_heads):
        q_part = q_rows[:, kv_head * groups * head_size:(kv_head + 1) * groups * head_size].reshape(row_count, groups, head_size)
        k_part = key_rows[:, kv_head * head_size:(kv_head + 1) * head_size]
        v_part = key_rows[:, (kv_heads + kv_head) * head_size:(kv_heads + kv_head + 1) * head_size]
        scores = jnp.einsum('tgd,ld->gtl', q_part.astype(jnp.float32), k_part.astype(jnp.float32)) * score_scale
        scores = jnp.where(visible[None], scores, -1e+30)
        row_max = lax.optimization_barrier(jnp.max(scores, axis=-1, keepdims=True))
        weights = jnp.exp(scores - row_max)
        totals = lax.optimization_barrier(jnp.sum(weights, axis=-1, keepdims=True))
        probs = weights.astype(jnp.bfloat16)
        mixed = jnp.einsum('gtl,ld->gtd', probs.astype(jnp.float32), v_part.astype(jnp.float32)) / totals
        outputs.append(mixed.astype(jnp.bfloat16).transpose(1, 0, 2).reshape(row_count, groups * head_size))
    return jnp.concatenate(outputs, axis=1)

def ssd_block(x_part, dt_part, bc_part, decay_rate, skip_gain, kept_state):
    state_count = bc_part.shape[-1] // 2
    b_part = bc_part[..., :state_count].astype(jnp.float32)
    c_part = bc_part[..., state_count:].astype(jnp.float32)
    dt_val = dt_part.astype(jnp.float32)
    cumulative = jnp.cumsum(dt_val * decay_rate, axis=1)
    inner_prod = jnp.einsum('rtn,rsn->rts', c_part, b_part)
    length = x_part.shape[1]
    causal = jnp.arange(length)[:, None] >= jnp.arange(length)[None, :]
    differences = cumulative[:, :, None, :] - cumulative[:, None, :, :]
    decays = jnp.exp(jnp.where(causal[None, :, :, None], differences, -jnp.inf))
    weights = (decays * inner_prod[..., None] * dt_val[:, None, :, :]).astype(jnp.bfloat16)
    x_float = x_part.astype(jnp.float32)
    within = jnp.einsum('rtsh,rshp->rthp', weights.astype(jnp.float32), x_float)
    carried = jnp.exp(cumulative)[..., None] * jnp.einsum('rtn,rhpn->rthp', c_part, kept_state, precision=lax.Precision.HIGHEST)
    output = within + carried + skip_gain[None, None, :, None] * x_float
    to_end = jnp.exp(cumulative[:, -1:, :] - cumulative) * dt_val
    weighted = (x_float * to_end[..., None]).astype(jnp.bfloat16)
    final_state = jnp.einsum('rshp,rsn->rhpn', weighted.astype(jnp.float32), b_part) + jnp.exp(cumulative[:, -1, :])[:, :, None, None] * kept_state
    return (output.astype(jnp.bfloat16), final_state)

def reference(x_rows, dt_rows, bc_rows, a_log, d_skip, state_pool, owners, queries, new_kv, page_pool, page_table, prefix_len):
    decay_rate = -jnp.exp(a_log)
    req_ids = jnp.arange(REQS, dtype=jnp.int32)

    def one_state(req_index):
        row_start = req_index * NEW
        x_part = lax.dynamic_slice_in_dim(x_rows, row_start, NEW, 0).reshape(1, NEW, MIXER_HEADS, P_SIZE)
        dt_part = lax.dynamic_slice_in_dim(dt_rows, row_start, NEW, 0).reshape(1, NEW, MIXER_HEADS)
        bc_part = lax.dynamic_slice_in_dim(bc_rows, row_start, NEW, 0).reshape(1, NEW, 2 * N)
        kept_state = jnp.take(state_pool, owners[req_index], axis=0)[None]
        output, final_state = ssd_block(x_part, dt_part, bc_part, decay_rate, d_skip, kept_state)
        return (output.reshape(NEW, MIXER_HEADS * P_SIZE), final_state[0])
    outputs, finals = lax.map(one_state, req_ids)
    ssd_out = outputs.reshape(TOKEN_TOTAL, MIXER_HEADS * P_SIZE)

    def one_attention(req_index):
        row_start = req_index * NEW
        q_rows = lax.dynamic_slice_in_dim(queries, row_start, NEW, 0)
        fresh_rows = lax.dynamic_slice_in_dim(new_kv, row_start, NEW, 0)
        page_base = req_index // REQ * (N_DEV * PG_DEV)
        page_ids = (page_table[req_index] + page_base).astype(jnp.int32)
        prefix_rows = jnp.take(page_pool, page_ids, axis=0).reshape(PREFIX, 2 * KVH * HD)
        before = jnp.arange(PREFIX, dtype=jnp.int32) < prefix_len[req_index]
        position = jnp.arange(NEW, dtype=jnp.int32)
        causal = position[None, :] <= position[:, None]
        visible = jnp.concatenate([jnp.broadcast_to(before[None, :], (NEW, PREFIX)), causal], axis=1)
        key_rows = jnp.concatenate([prefix_rows, fresh_rows], axis=0)
        return attend(q_rows, key_rows, visible, KVH, HD)
    attn_values = lax.map(one_attention, req_ids).reshape(TOKEN_TOTAL, QH * HD)
    return (ssd_out, finals, attn_values)
```

```python
import math

import jax
import jax.numpy as jnp
from jax import lax
from jax.experimental import pallas as pl
from jax.experimental.pallas import tpu as pltpu
from jax.sharding import PartitionSpec as P

MESH = pl.DeviceIdType.MESH
F32, BF16 = jnp.float32, jnp.bfloat16
NX, NZ, NC, NG = 4, 8, 2, 4
NDEV = NX * NZ * NC
REQ = 32
TOK = 128
NEW = 2 * TOK
HEADS_CORE = 4
QPER = 4
PAGE = 16
PREFIX = 1024
HALF = HEADS_CORE * 128
QHALF = HEADS_CORE * QPER * 128
PHASES = 2
PER_PHASE = HEADS_CORE // PHASES
EXP2_SCALE = math.log2(math.e) / math.sqrt(128.0)
HIDDEN = -1e30

NT = (((1,), (1,)), ((), ()))
TN = (((0,), (0,)), ((), ()))


def dot(a, b, dims=(((1,), (0,)), ((), ())), precision=None):
    return lax.dot_general(a, b, dims, precision=precision, preferred_element_type=F32)


def kernel(
    slots,
    owners,
    a_log,
    d_skip,
    bias,
    dt_in,
    x_in,
    bc_in,
    pool_in,
    q_in,
    kv_in,
    pages_in,
    ssd_hbm,
    fin_hbm,
    attn_hbm,
    xbuf,
    dtbuf,
    bcbuf,
    states,
    stage,
    kvbuf,
    qbuf,
    newbuf,
    obuf,
    by_req,
    dt_rows,
    ssd_v,
    fin_v,
    recv,
    send,
    recv_x,
    recv_c,
    recv_kv,
    send_kv,
    out_sem,
):
    grp = lax.axis_index("grp")
    me = lax.axis_index("dev")
    myx, myz, myc = lax.div(me, NZ * NC), lax.rem(lax.div(me, NC), NZ), lax.rem(me, NC)
    other = me + 1 - 2 * myc

    def peer(step):
        x = lax.rem(myx + lax.div(step, NZ * NC), NX)
        z = lax.rem(myz + lax.div(step, NC), NZ)
        return (x * NZ + z) * NC + lax.rem(myc + step, NC)

    def remote(src, dst, send_sem, recv_sem, where):
        return pltpu.make_async_remote_copy(
            src_ref=src,
            dst_ref=dst,
            send_sem=send_sem,
            recv_sem=recv_sem,
            device_id=where,
            device_id_type=MESH,
        )

    def wait_for(ref, sem):
        pltpu.make_async_copy(ref, ref, sem).wait()

    R_X, R_DT, R_ST, R_Q, R_NK, R_BC, R_OUT = range(7)
    S_X, S_DT, S_ST, S_Q, S_NK, S_BC, S_BX, S_CORE, S_OUT = range(9)

    barrier = pltpu.get_barrier_semaphore()

    @pl.loop(1, NDEV)
    def _(step):
        pl.semaphore_signal(barrier, inc=1, device_id={"dev": peer(step)}, device_id_type=MESH)

    for dg in range(1, NG):
        pl.semaphore_signal(
            barrier, inc=1, device_id={"grp": (grp + dg) % NG}, device_id_type=MESH
        )

    states[grp] = pool_in[...].astype(BF16)

    @pl.loop(0, REQ)
    def _(r):
        slot = slots[r]
        for kv in range(2):
            for head in range(2 * HEADS_CORE):
                c, hh = head // HEADS_CORE, head % HEADS_CORE
                col = (kv * 2 * HEADS_CORE + head) * 128
                stage[hh // PER_PHASE, 2 * r + c, hh % PER_PHASE, kv] = pages_in[
                    slot, :, col : col + 128
                ]

    pl.semaphore_wait(barrier, NDEV - 1 + NG - 1)

    pltpu.make_async_copy(bc_in, bcbuf.at[myx, myc, myz], recv.at[R_BC]).start()
    for dz in range(1, NZ):
        to = (myx * NZ + (myz + dz) % NZ) * NC + myc
        remote(
            bc_in, bcbuf.at[myx, myc, myz], send.at[S_BC], recv.at[R_BC], {"dev": to}
        ).start()

    for dg in range(1, NG):
        remote(
            states.at[grp],
            states.at[grp],
            send.at[S_ST],
            recv.at[R_ST],
            {"grp": (grp + dg) % NG},
        ).start()

    pltpu.make_async_copy(
        x_in.at[:, pl.ds(pl.multiple_of(me * 128, 128), 128)], xbuf.at[me], recv.at[R_X]
    ).start()
    pltpu.make_async_copy(dt_in.at[me], dtbuf.at[me], recv.at[R_DT]).start()

    @pl.loop(1, NDEV)
    def _(step):
        to = peer(step)
        remote(
            x_in.at[:, pl.ds(pl.multiple_of(to * 128, 128), 128)],
            xbuf.at[me],
            send.at[S_X],
            recv.at[R_X],
            {"dev": to},
        ).start()
        remote(dt_in.at[to], dtbuf.at[me], send.at[S_DT], recv.at[R_DT], {"dev": to}).start()

    my_rows = pl.ds(pl.multiple_of(myc * TOK, TOK), TOK)

    def half(ref, start, width, core):
        return ref.at[:, pl.ds(pl.multiple_of(start + core * width, width), width)]

    pltpu.make_async_copy(half(q_in, 0, QHALF, myc), qbuf.at[my_rows], recv.at[R_Q]).start()
    remote(
        half(q_in, 0, QHALF, 1 - myc),
        qbuf.at[my_rows],
        send.at[S_Q],
        recv.at[R_Q],
        {"dev": other},
    ).start()
    for kv in range(2):
        pltpu.make_async_copy(
            half(kv_in, kv * 2 * HALF, HALF, myc), newbuf.at[kv, my_rows], recv.at[R_NK]
        ).start()
        remote(
            half(kv_in, kv * 2 * HALF, HALF, 1 - myc),
            newbuf.at[kv, my_rows],
            send.at[S_NK],
            recv.at[R_NK],
            {"dev": other},
        ).start()

    wait_for(bcbuf.at[myx, myc], recv.at[R_BC])
    for dx in range(1, NX):
        to = (((myx + dx) % NX) * NZ + myz) * NC + myc
        remote(
            bcbuf.at[myx, myc],
            bcbuf.at[myx, myc],
            send.at[S_BX],
            recv_x.at[dx],
            {"dev": to},
        ).start()
    for dx in range(NX):
        block = bcbuf.at[(myx + NX - dx) % NX, myc]
        if dx:
            wait_for(block, recv_x.at[dx])
        remote(block, block, send.at[S_CORE], recv_c.at[dx], {"dev": other}).start()

    wait_for(xbuf, recv.at[R_X])

    for p in range(PHASES):
        mine = kvbuf.at[pl.ds(p * PER_PHASE, PER_PHASE), :, me]
        pltpu.make_async_copy(stage.at[p, me], mine, recv_kv.at[p]).start()

        @pl.loop(1, NDEV)
        def _(step):
            to = peer(step)
            remote(
                stage.at[p, to], mine, send_kv.at[p], recv_kv.at[p], {"dev": to}
            ).start()

    wait_for(dtbuf, recv.at[R_DT])
    wait_for(states.at[pl.ds(0, NG - 1)], recv.at[R_ST])
    for dx in range(NX):
        wait_for(bcbuf.at[(myx + NX - dx) % NX, 1 - myc], recv_c.at[dx])

    for r in range(REQ):
        for c in range(NC):
            piece = dtbuf[2 * r + c]
            dt_rows[2 * r : 2 * r + 2, c * TOK : (c + 1) * TOK] = piece
            by_req[r, 2:4, c * TOK : (c + 1) * TOK] = piece
    odd_row = lax.broadcasted_iota(jnp.int32, (2 * REQ, NEW), 0) % 2 == 1
    rate = -jnp.exp(
        jnp.where(odd_row, jnp.full((2 * REQ, NEW), a_log[1]), jnp.full((2 * REQ, NEW), a_log[0]))
    )
    earlier = lax.broadcasted_iota(jnp.int32, (NEW, NEW), 0)
    later = lax.broadcasted_iota(jnp.int32, (NEW, NEW), 1)
    cumulative = dot(
        dt_rows[...] * rate,
        (earlier <= later).astype(F32),
        precision=lax.Precision.HIGHEST,
    )
    for r in range(REQ):
        by_req[r, 0:2, :] = cumulative[2 * r : 2 * r + 2]

    second = lax.broadcasted_iota(jnp.int32, (1, 128), 1) >= 64
    skip = jnp.where(second, jnp.full((1, 128), d_skip[1]), jnp.full((1, 128), d_skip[0]))
    low_half = lax.broadcasted_iota(jnp.int32, (128, 1), 0) < 64
    diagonal = lax.broadcasted_iota(jnp.int32, (TOK, TOK), 0) >= lax.broadcasted_iota(
        jnp.int32, (TOK, TOK), 1
    )

    @pl.loop(0, REQ)
    def _(r):
        rx, rz = lax.div(r, NZ), lax.rem(r, NZ)
        x = jnp.concatenate([xbuf[2 * r], xbuf[2 * r + 1]], axis=0)
        bc = jnp.concatenate([bcbuf[rx, 0, rz], bcbuf[rx, 1, rz]], axis=0)
        b, c = bc[:, :128], bc[:, 128:]
        kept = states[lax.div(owners[r], 16), lax.rem(owners[r], 16)]
        cum = by_req[r, 0:2, :]
        dt = by_req[r, 2:4, :]
        last = cum[:, NEW - 1 :]
        to_end = jnp.exp(last - cum) * dt
        from_start = jnp.exp(cum)
        columns = jnp.concatenate([cum, from_start, to_end, cum], axis=0).T
        inner = dot(c, b, NT)
        zero = jnp.zeros((TOK, TOK), BF16)
        weights = []
        for h in range(2):
            blocks = {}
            for i, j in ((0, 0), (1, 0), (1, 1)):
                rows, cols = slice(i * TOK, (i + 1) * TOK), slice(j * TOK, (j + 1) * TOK)
                diff = columns[rows, h : h + 1] - cum[h : h + 1, cols]
                if i == j:
                    diff = jnp.where(diagonal, diff, -jnp.inf)
                blocks[i, j] = (jnp.exp(diff) * inner[rows, cols] * dt[h : h + 1, cols]).astype(
                    BF16
                )
            weights.append(
                jnp.concatenate(
                    [
                        jnp.concatenate([blocks[0, 0], zero], axis=1),
                        jnp.concatenate([blocks[1, 0], blocks[1, 1]], axis=1),
                    ],
                    axis=0,
                )
            )
        x_first = jnp.where(second, jnp.zeros_like(x), x)
        x_second = jnp.where(second, x, jnp.zeros_like(x))
        within = dot(weights[0], x_first) + dot(weights[1], x_second)
        x_float = x.astype(F32)
        growth = jnp.where(second, columns[:, 3:4], columns[:, 2:3])
        carried = growth * dot(c, kept, NT)
        ssd_v[pl.ds(pl.multiple_of(r * NEW, NEW), NEW), :] = (
            within + carried + skip * x_float
        ).astype(BF16)
        gain = jnp.where(second, columns[:, 5:6], columns[:, 4:5])
        weighted = (x_float * gain).astype(BF16)
        total = jnp.exp(last)
        left = jnp.where(
            low_half,
            jnp.broadcast_to(total[0:1], (128, 1)),
            jnp.broadcast_to(total[1:2], (128, 1)),
        )
        fin_v[r] = dot(weighted, b, TN) + left * kept.astype(F32)

    pltpu.make_async_copy(ssd_v, ssd_hbm, out_sem.at[0]).start()
    pltpu.make_async_copy(fin_v, fin_hbm, out_sem.at[1]).start()

    wait_for(qbuf, recv.at[R_Q])
    wait_for(newbuf, recv.at[R_NK])
    causal = lax.broadcasted_iota(jnp.int32, (NEW, NEW), 0) >= lax.broadcasted_iota(
        jnp.int32, (NEW, NEW), 1
    )
    for p in range(PHASES):
        wait_for(kvbuf.at[pl.ds(p * PER_PHASE, PER_PHASE)], recv_kv.at[p])

        @pl.loop(p * PER_PHASE * QPER, (p + 1) * PER_PHASE * QPER)
        def _(qh):
            h = lax.div(qh, QPER)
            head_cols = pl.ds(pl.multiple_of(h * 128, 128), 128)
            q = qbuf[:, pl.ds(pl.multiple_of(qh * 128, 128), 128)]
            keys = kvbuf[h, 0].reshape(PREFIX, 128)
            values = kvbuf[h, 1].reshape(PREFIX, 128)
            old = dot(q, keys, NT) + bias[...]
            new = jnp.where(causal, dot(q, newbuf[0, :, head_cols], NT), HIDDEN)
            top = jnp.maximum(
                jnp.max(old, axis=1, keepdims=True), jnp.max(new, axis=1, keepdims=True)
            )
            shift = top * EXP2_SCALE
            old = jnp.exp2(old * EXP2_SCALE - shift)
            new = jnp.exp2(new * EXP2_SCALE - shift)
            totals = jnp.sum(old, axis=1, keepdims=True) + jnp.sum(new, axis=1, keepdims=True)
            mixed = dot(old.astype(BF16), values) + dot(
                new.astype(BF16), newbuf[1, :, head_cols]
            )
            obuf[:, pl.ds(pl.multiple_of(qh * 128, 128), 128)] = (mixed / totals).astype(BF16)

        width = QHALF // PHASES
        src_cols = pl.ds(p * width, width)
        dst_cols = pl.ds(pl.multiple_of(myc * QHALF + p * width, width), width)
        pltpu.make_async_copy(
            obuf.at[my_rows, src_cols], attn_hbm.at[:, dst_cols], recv.at[R_OUT]
        ).start()
        remote(
            obuf.at[pl.ds(pl.multiple_of((1 - myc) * TOK, TOK), TOK), src_cols],
            attn_hbm.at[:, dst_cols],
            send.at[S_OUT],
            recv.at[R_OUT],
            {"dev": other},
        ).start()

    wait_for(ssd_v, out_sem.at[0])
    wait_for(fin_v, out_sem.at[1])
    wait_for(attn_hbm, recv.at[R_OUT])
    rest = pl.ds(0, NDEV - 1)
    wait_for(xbuf.at[rest], send.at[S_X])
    wait_for(dtbuf.at[rest], send.at[S_DT])
    wait_for(states.at[pl.ds(0, NG - 1)], send.at[S_ST])
    wait_for(qbuf.at[pl.ds(0, TOK)], send.at[S_Q])
    wait_for(newbuf.at[0], send.at[S_NK])
    wait_for(bcbuf.at[0, 0, pl.ds(0, NZ - 1)], send.at[S_BC])
    wait_for(bcbuf.at[pl.ds(0, NX - 1), 0], send.at[S_BX])
    wait_for(bcbuf.at[:, 0], send.at[S_CORE])
    wait_for(obuf.at[pl.ds(0, TOK)], send.at[S_OUT])
    for p in range(PHASES):
        wait_for(stage.at[p, rest], send_kv.at[p])


def on_device(
    x_rows,
    dt_rows,
    bc_rows,
    a_log,
    d_skip,
    state_pool,
    owners,
    queries,
    new_kv,
    page_pool,
    page_table,
    prefix_len,
):
    me = lax.axis_index("dev")
    pages_here = page_pool.shape[0]
    holder, place = page_table // pages_here, page_table % pages_here
    slots = jnp.sum(jnp.where(holder == me, place, 0), axis=1)
    my_holder = lax.dynamic_index_in_dim(holder, me // NC, 0, keepdims=False)
    block = jnp.arange(NDEV, dtype=jnp.int32)
    at = jnp.sum(jnp.where(my_holder[None, :] == block[:, None], block[None, :], 0), axis=1)
    position = at[:, None] * PAGE + jnp.arange(PAGE, dtype=jnp.int32)[None, :]
    my_len = lax.dynamic_index_in_dim(prefix_len, me // NC, 0, keepdims=False)
    bias = jnp.where(position < my_len, 0.0, HIDDEN).astype(F32).reshape(1, PREFIX)
    dt_sent = dt_rows.astype(F32).T.reshape(NDEV, 2, TOK)
    smem = pl.BlockSpec(memory_space=pltpu.SMEM)
    vmem = pl.BlockSpec(memory_space=pltpu.VMEM)
    hbm = pl.BlockSpec(memory_space=pl.ANY)
    dma = pltpu.SemaphoreType.DMA
    ssd_out, finals, attn_out = pl.pallas_call(
        kernel,
        out_shape=(
            jax.ShapeDtypeStruct((REQ * NEW, 128), BF16),
            jax.ShapeDtypeStruct((REQ, 128, 128), F32),
            jax.ShapeDtypeStruct((TOK, 2 * QHALF), BF16),
        ),
        in_specs=[smem] * 4 + [vmem, hbm, hbm, hbm, vmem, hbm, hbm, vmem],
        out_specs=(hbm, hbm, hbm),
        scratch_shapes=[
            pltpu.VMEM((NDEV, TOK, 128), BF16),
            pltpu.VMEM((NDEV, 2, TOK), F32),
            pltpu.VMEM((NX, NC, NZ, TOK, 256), BF16),
            pltpu.VMEM((NG, 16, 128, 128), BF16),
            pltpu.VMEM((PHASES, NDEV, PER_PHASE, 2, PAGE, 128), BF16),
            pltpu.VMEM((HEADS_CORE, 2, NDEV, PAGE, 128), BF16),
            pltpu.VMEM((NEW, QHALF), BF16),
            pltpu.VMEM((2, NEW, HALF), BF16),
            pltpu.VMEM((NEW, QHALF), BF16),
            pltpu.VMEM((REQ, 8, NEW), F32),
            pltpu.VMEM((2 * REQ, NEW), F32),
            pltpu.VMEM((REQ * NEW, 128), BF16),
            pltpu.VMEM((REQ, 128, 128), F32),
            dma((7,)),
            dma((9,)),
            dma((NX,)),
            dma((NX,)),
            dma((PHASES,)),
            dma((PHASES,)),
            dma((2,)),
        ],
        compiler_params=pltpu.CompilerParams(
            collective_id=0, has_side_effects=True, vmem_limit_bytes=56 * 1024 * 1024
        ),
    )(
        slots,
        owners,
        a_log,
        d_skip,
        bias,
        dt_sent,
        x_rows,
        bc_rows,
        state_pool.reshape(16, 128, 128),
        queries,
        new_kv,
        page_pool,
    )
    return ssd_out, finals.reshape(REQ, 2, 64, 128), attn_out


def solution(mesh):
    return jax.shard_map(
        on_device,
        mesh=mesh,
        in_specs=(
            P(("grp", "dev"), None),
            P(("grp", "dev"), None),
            P(("grp", "dev"), None),
            P("dev"),
            P("dev"),
            P("grp", "dev", None, None),
            P("grp"),
            P(("grp", "dev"), None),
            P(("grp", "dev"), None),
            P(("grp", "dev"), None, None),
            P("grp", None),
            P("grp"),
        ),
        out_specs=(P("grp", "dev"), P("grp", "dev", None, None), P(("grp", "dev"), None)),
        check_vma=False,
    )
```

```python
import math

import jax
import jax.numpy as jnp
from jax import lax
from jax.experimental import pallas as pl
from jax.experimental.pallas import tpu as pltpu
from jax.sharding import PartitionSpec as P

MESH = pl.DeviceIdType.MESH
F32, BF16 = jnp.float32, jnp.bfloat16
NX, NZ, NC, NG = 4, 8, 2, 4
NDEV = NX * NZ * NC
REQ = 32
TOK = 128
NEW = 2 * TOK
HEADS_CORE = 4
QPER = 4
PAGE = 16
HELD = 8
PARTS = 2
ROUTES = 9
PREFIX = 1024
HALF = HEADS_CORE * 128
QHALF = HEADS_CORE * QPER * 128
PHASES = 2
PER_PHASE = HEADS_CORE // PHASES
EXP2_SCALE = math.log2(math.e) / math.sqrt(128.0)
HIDDEN = -1e30

NT = (((1,), (1,)), ((), ()))
TN = (((0,), (0,)), ((), ()))


def dot(a, b, dims=(((1,), (0,)), ((), ())), precision=None):
    return lax.dot_general(a, b, dims, precision=precision, preferred_element_type=F32)


def kernel(
    slots,
    owners,
    a_log,
    d_skip,
    bias,
    dt_in,
    x_in,
    bc_in,
    pool_in,
    q_in,
    kv_in,
    pages_in,
    ssd_hbm,
    fin_hbm,
    attn_hbm,
    xbuf,
    dtbuf,
    bcbuf,
    states,
    pool_own,
    up_near,
    up_far,
    down_near,
    down_far,
    stage,
    kvbuf,
    qbuf,
    newbuf,
    obuf,
    by_req,
    dt_rows,
    ssd_v,
    fin_v,
    recv,
    send,
    ring_bc,
    ring_pg,
    recv_x,
    recv_bx,
    recv_c,
    out_sem,
):
    grp = lax.axis_index("grp")
    me = lax.axis_index("dev")
    myx, myz, myc = lax.div(me, NZ * NC), lax.rem(lax.div(me, NC), NZ), lax.rem(me, NC)
    other = me + 1 - 2 * myc

    def peer(step):
        x = lax.rem(myx + lax.div(step, NZ * NC), NX)
        z = lax.rem(myz + lax.div(step, NC), NZ)
        return (x * NZ + z) * NC + lax.rem(myc + step, NC)

    def remote(src, dst, send_sem, recv_sem, where):
        return pltpu.make_async_remote_copy(
            src_ref=src,
            dst_ref=dst,
            send_sem=send_sem,
            recv_sem=recv_sem,
            device_id=where,
            device_id_type=MESH,
        )

    def wait_for(ref, sem):
        pltpu.make_async_copy(ref, ref, sem).wait()

    R_DT, R_ST, R_Q, R_NK, R_BC, R_PG, R_KV, R_OUT = range(8)
    S_X, S_DT, S_ST, S_Q, S_NK, S_BC, S_PG, S_BX, S_KV, S_CORE, S_OUT = range(11)

    barrier = pltpu.get_barrier_semaphore()

    @pl.loop(1, NDEV)
    def _(step):
        pl.semaphore_signal(barrier, inc=1, device_id={"dev": peer(step)}, device_id_type=MESH)

    for dg in range(1, NG):
        pl.semaphore_signal(
            barrier, inc=1, device_id={"grp": (grp + dg) % NG}, device_id_type=MESH
        )

    states[grp] = pool_in[...].astype(BF16)

    pl.semaphore_wait(barrier, NDEV - 1 + NG - 1)

    for dg in range(1, NG):
        remote(
            states.at[grp],
            states.at[grp],
            send.at[S_ST],
            recv.at[R_ST],
            {"grp": lax.rem(grp + dg, NG)},
        ).start()

    def on_ring(dz):
        return lax.rem(myz + dz + NZ, NZ)

    def at(x, z, c):
        return {"dev": (x * NZ + z) * NC + c}

    def map_rows(side):
        return pl.ds(side * (TOK // 2), TOK // 2)

    def page_rows(part):
        return pl.ds(part * (HELD // PARTS), HELD // PARTS)

    ways = (1, -1)
    held = ((up_near, up_far), (down_near, down_far))

    def pass_maps(step, side, source, distance=1, rows=None):
        block = bcbuf.at[myx, myc, on_ring(-min(step - 1, 2) * ways[side])]
        if rows is not None:
            block = block.at[rows]
        remote(
            block if source is None else source,
            block,
            send.at[S_BC],
            ring_bc.at[side, step - 1],
            at(myx, on_ring(distance * ways[side]), myc),
        ).start()

    def pass_pages(step, side, part):
        source = pages_in if step == 1 else held[side][0]
        remote(
            source.at[page_rows(part)],
            held[side][step - 1].at[page_rows(part)],
            send.at[S_PG],
            ring_pg.at[side, step - 1, part],
            at(myx, on_ring(ways[side]), myc),
        ).start()

    for side in range(2):
        pass_maps(1, side, bc_in)
    for part in range(PARTS):
        for side in range(2):
            pass_pages(1, side, part)
    own_pages = pltpu.make_async_copy(pages_in, pool_own, recv.at[R_PG])
    own_pages.start()
    own_maps = pltpu.make_async_copy(bc_in, bcbuf.at[myx, myc, myz], recv.at[R_BC])
    own_maps.start()

    def send_x(dz, k):
        x = lax.rem(myx + lax.div(k, NC), NX)
        to = (x * NZ + lax.rem(myz + dz, NZ)) * NC + lax.rem(myc + k, NC)
        remote(
            x_in.at[:, pl.ds(pl.multiple_of(to * 128, 128), 128)],
            xbuf.at[myz, myx, myc],
            send.at[S_X],
            recv_x.at[dz],
            {"dev": to},
        ).start()

    pltpu.make_async_copy(
        x_in.at[:, pl.ds(pl.multiple_of(me * 128, 128), 128)],
        xbuf.at[myz, myx, myc],
        recv_x.at[0],
    ).start()
    pltpu.make_async_copy(dt_in.at[me], dtbuf.at[myz, myx, myc], recv.at[R_DT]).start()

    @pl.loop(1, NX * NC)
    def _(k):
        send_x(0, k)

    @pl.loop(1, NDEV)
    def _(step):
        to = peer(step)
        remote(
            dt_in.at[to], dtbuf.at[myz, myx, myc], send.at[S_DT], recv.at[R_DT], {"dev": to}
        ).start()

    def send_both_ways(near):
        @pl.loop(0, 2 * NX * NC)
        def _(i):
            send_x(near + lax.rem(i, 2) * (NZ - 2 * near), lax.div(i, 2))

    def send_far():
        @pl.loop(0, NX * NC)
        def _(k):
            send_x(4, k)

    my_rows = pl.ds(pl.multiple_of(myc * TOK, TOK), TOK)

    def half(ref, start, width, core):
        return ref.at[:, pl.ds(pl.multiple_of(start + core * width, width), width)]

    pltpu.make_async_copy(half(q_in, 0, QHALF, myc), qbuf.at[my_rows], recv.at[R_Q]).start()
    remote(
        half(q_in, 0, QHALF, 1 - myc),
        qbuf.at[my_rows],
        send.at[S_Q],
        recv.at[R_Q],
        {"dev": other},
    ).start()
    for kv in range(2):
        pltpu.make_async_copy(
            half(kv_in, kv * 2 * HALF, HALF, myc), newbuf.at[kv, my_rows], recv.at[R_NK]
        ).start()
        remote(
            half(kv_in, kv * 2 * HALF, HALF, 1 - myc),
            newbuf.at[kv, my_rows],
            send.at[S_NK],
            recv.at[R_NK],
            {"dev": other},
        ).start()

    def spread_maps(z):
        block = bcbuf.at[myx, myc, z]
        for dx in range(1, NX):
            remote(
                block,
                block,
                send.at[S_BX],
                recv_bx.at[dx],
                at(lax.rem(myx + dx, NX), myz, myc),
            ).start()

    def spread_pages(place, pages, away, onward=0, cores=(0, 1)):
        z, target = on_ring(away), on_ring(onward)
        mine = kvbuf.at[:, :, myx, myc, z]

        @pl.loop(0, NX)
        def _(x):
            slot = slots[(x * NZ + target) * NZ + z]
            for kv in range(2):
                for c in cores:
                    for hh in range(HEADS_CORE):
                        col = ((kv * 2 + c) * HEADS_CORE + hh) * 128
                        stage[place, x, c, hh, kv] = pages[slot, :, col : col + 128]

        def pages_to(x, c):
            remote(
                stage.at[place, x, c], mine, send.at[S_KV], recv.at[R_KV], at(x, target, c)
            ).start()

        if onward == 0:
            pltpu.make_async_copy(stage.at[place, myx, myc], mine, recv.at[R_KV]).start()

            @pl.loop(1, NX * NC)
            def _(k):
                pages_to(lax.rem(myx + lax.div(k, NC), NX), lax.rem(myc + k, NC))
        elif len(cores) == 2:

            @pl.loop(0, NX * NC)
            def _(k):
                pages_to(lax.rem(myx + lax.div(k, NC), NX), lax.rem(myc + k, NC))
        else:

            @pl.loop(0, NX)
            def _(dx):
                pages_to(lax.rem(myx + dx, NX), cores[0])

    own_maps.wait()
    spread_maps(myz)
    own_pages.wait()
    spread_pages(0, pool_own, 0)
    for step in (1, 2):
        for side in range(2):
            z = on_ring(-step * ways[side])
            wait_for(bcbuf.at[myx, myc, z], ring_bc.at[side, step - 1])
            pass_maps(step + 1, side, None)
            if step == 2:
                pass_maps(4, side, None, 2, map_rows(side))
        for part in range(PARTS):
            for side in range(2):
                wait_for(
                    held[side][step - 1].at[page_rows(part)], ring_pg.at[side, step - 1, part]
                )
                if step == 1:
                    pass_pages(2, side, part)
        for side in range(2):
            spread_maps(on_ring(-step * ways[side]))
        if step == 2:
            for side in range(2):
                spread_pages(5 + side, held[side][1], -2 * ways[side], 2 * ways[side], (side,))
            for side in range(2):
                spread_pages(7 + side, held[side][1], -2 * ways[side], ways[side])
        for side in range(2):
            spread_pages(2 * step - 1 + side, held[side][step - 1], -step * ways[side])

    for side in range(2):
        z = on_ring(-3 * ways[side])
        wait_for(bcbuf.at[myx, myc, z], ring_bc.at[side, 2])
        spread_maps(z)
    far = on_ring(4)
    for side in range(2):
        wait_for(bcbuf.at[myx, myc, far, map_rows(side)], ring_bc.at[side, 3])
    spread_maps(far)
    send_far()
    send_both_ways(3)

    def maps_to_other_core():
        for dx in range(NX):
            block = bcbuf.at[lax.rem(myx + NX - dx, NX), myc]
            if dx:
                wait_for(block, recv_bx.at[dx])
            remote(block, block, send.at[S_CORE], recv_c.at[dx], {"dev": other}).start()

    maps_to_other_core()
    send_both_ways(2)
    send_both_ways(1)
    wait_for(qbuf, recv.at[R_Q])
    wait_for(newbuf, recv.at[R_NK])
    wait_for(kvbuf, recv.at[R_KV])
    causal = lax.broadcasted_iota(jnp.int32, (NEW, NEW), 0) >= lax.broadcasted_iota(
        jnp.int32, (NEW, NEW), 1
    )
    for p in range(PHASES):
        @pl.loop(p * PER_PHASE * QPER, (p + 1) * PER_PHASE * QPER)
        def _(qh):
            h = lax.div(qh, QPER)
            head_cols = pl.ds(pl.multiple_of(h * 128, 128), 128)
            q = qbuf[:, pl.ds(pl.multiple_of(qh * 128, 128), 128)]
            keys = kvbuf[h, 0].reshape(PREFIX, 128)
            values = kvbuf[h, 1].reshape(PREFIX, 128)
            old = dot(q, keys, NT) + bias[...]
            new = jnp.where(causal, dot(q, newbuf[0, :, head_cols], NT), HIDDEN)
            top = jnp.maximum(
                jnp.max(old, axis=1, keepdims=True), jnp.max(new, axis=1, keepdims=True)
            )
            shift = top * EXP2_SCALE
            old = jnp.exp2(old * EXP2_SCALE - shift)
            new = jnp.exp2(new * EXP2_SCALE - shift)
            totals = jnp.sum(old, axis=1, keepdims=True) + jnp.sum(new, axis=1, keepdims=True)
            mixed = dot(old.astype(BF16), values) + dot(
                new.astype(BF16), newbuf[1, :, head_cols]
            )
            obuf[:, pl.ds(pl.multiple_of(qh * 128, 128), 128)] = (mixed / totals).astype(BF16)

        width = QHALF // PHASES
        src_cols = pl.ds(p * width, width)
        dst_cols = pl.ds(pl.multiple_of(myc * QHALF + p * width, width), width)
        pltpu.make_async_copy(
            obuf.at[my_rows, src_cols], attn_hbm.at[:, dst_cols], recv.at[R_OUT]
        ).start()
        remote(
            obuf.at[pl.ds(pl.multiple_of((1 - myc) * TOK, TOK), TOK), src_cols],
            attn_hbm.at[:, dst_cols],
            send.at[S_OUT],
            recv.at[R_OUT],
            {"dev": other},
        ).start()

    wait_for(dtbuf, recv.at[R_DT])
    wait_for(states.at[pl.ds(0, NG - 1)], recv.at[R_ST])
    for dx in range(NX):
        wait_for(bcbuf.at[lax.rem(myx + NX - dx, NX), 1 - myc], recv_c.at[dx])

    for r in range(REQ):
        for c in range(NC):
            piece = dtbuf[r % NZ, r // NZ, c]
            dt_rows[2 * r : 2 * r + 2, c * TOK : (c + 1) * TOK] = piece
            by_req[r, 2:4, c * TOK : (c + 1) * TOK] = piece
    odd_row = lax.broadcasted_iota(jnp.int32, (2 * REQ, NEW), 0) % 2 == 1
    rate = -jnp.exp(
        jnp.where(odd_row, jnp.full((2 * REQ, NEW), a_log[1]), jnp.full((2 * REQ, NEW), a_log[0]))
    )
    earlier = lax.broadcasted_iota(jnp.int32, (NEW, NEW), 0)
    later = lax.broadcasted_iota(jnp.int32, (NEW, NEW), 1)
    cumulative = dot(
        dt_rows[...] * rate,
        (earlier <= later).astype(F32),
        precision=lax.Precision.HIGHEST,
    )
    for r in range(REQ):
        by_req[r, 0:2, :] = cumulative[2 * r : 2 * r + 2]

    second = lax.broadcasted_iota(jnp.int32, (1, 128), 1) >= 64
    skip = jnp.where(second, jnp.full((1, 128), d_skip[1]), jnp.full((1, 128), d_skip[0]))
    low_half = lax.broadcasted_iota(jnp.int32, (128, 1), 0) < 64
    diagonal = lax.broadcasted_iota(jnp.int32, (TOK, TOK), 0) >= lax.broadcasted_iota(
        jnp.int32, (TOK, TOK), 1
    )

    def ssd_request(rx, rz):
        r = rx * NZ + rz
        x = jnp.concatenate([xbuf[rz, rx, 0], xbuf[rz, rx, 1]], axis=0)
        bc = jnp.concatenate([bcbuf[rx, 0, rz], bcbuf[rx, 1, rz]], axis=0)
        b, c = bc[:, :128], bc[:, 128:]
        kept = states[lax.div(owners[r], 16), lax.rem(owners[r], 16)]
        cum = by_req[r, 0:2, :]
        dt = by_req[r, 2:4, :]
        last = cum[:, NEW - 1 :]
        to_end = jnp.exp(last - cum) * dt
        from_start = jnp.exp(cum)
        columns = jnp.concatenate([cum, from_start, to_end, cum], axis=0).T
        inner = dot(c, b, NT)
        zero = jnp.zeros((TOK, TOK), BF16)
        weights = []
        for h in range(2):
            blocks = {}
            for i, j in ((0, 0), (1, 0), (1, 1)):
                rows, cols = slice(i * TOK, (i + 1) * TOK), slice(j * TOK, (j + 1) * TOK)
                diff = columns[rows, h : h + 1] - cum[h : h + 1, cols]
                if i == j:
                    diff = jnp.where(diagonal, diff, -jnp.inf)
                blocks[i, j] = (jnp.exp(diff) * inner[rows, cols] * dt[h : h + 1, cols]).astype(
                    BF16
                )
            weights.append(
                jnp.concatenate(
                    [
                        jnp.concatenate([blocks[0, 0], zero], axis=1),
                        jnp.concatenate([blocks[1, 0], blocks[1, 1]], axis=1),
                    ],
                    axis=0,
                )
            )
        x_first = jnp.where(second, jnp.zeros_like(x), x)
        x_second = jnp.where(second, x, jnp.zeros_like(x))
        within = dot(weights[0], x_first) + dot(weights[1], x_second)
        x_float = x.astype(F32)
        growth = jnp.where(second, columns[:, 3:4], columns[:, 2:3])
        carried = growth * dot(c, kept, NT)
        rows = pl.ds(pl.multiple_of(r * NEW, NEW), NEW)
        ssd_v[rows, :] = (
            within + carried + skip * x_float
        ).astype(BF16)
        gain = jnp.where(second, columns[:, 5:6], columns[:, 4:5])
        weighted = (x_float * gain).astype(BF16)
        total = jnp.exp(last)
        left = jnp.where(
            low_half,
            jnp.broadcast_to(total[0:1], (128, 1)),
            jnp.broadcast_to(total[1:2], (128, 1)),
        )
        fin_v[r] = dot(weighted, b, TN) + left * kept.astype(F32)
        pltpu.make_async_copy(ssd_v.at[rows], ssd_hbm.at[rows], out_sem.at[0]).start()
        pltpu.make_async_copy(fin_v.at[r], fin_hbm.at[r], out_sem.at[1]).start()

    @pl.loop(0, NZ)
    def _(i):
        j = lax.rem(i + NZ - 1, NZ)
        odd = lax.rem(j, 2)
        dz = 4 + (1 - odd) * lax.div(j, 2) - odd * lax.div(j + 1, 2)
        rz = lax.rem(myz + NZ - dz, NZ)
        wait_for(xbuf.at[rz], recv_x.at[dz])

        @pl.loop(0, NX, unroll=2)
        def _(rx):
            ssd_request(rx, rz)

    wait_for(ssd_v, out_sem.at[0])
    wait_for(fin_v, out_sem.at[1])
    wait_for(attn_hbm, recv.at[R_OUT])
    wait_for(xbuf.at[pl.ds(0, NZ - 1)], send.at[S_X])
    wait_for(xbuf.at[0, pl.ds(0, NX - 1)], send.at[S_X])
    wait_for(xbuf.at[0, 0, 0], send.at[S_X])
    wait_for(dtbuf.at[pl.ds(0, NZ - 1)], send.at[S_DT])
    wait_for(dtbuf.at[0, pl.ds(0, NX - 1)], send.at[S_DT])
    wait_for(dtbuf.at[0, 0, 0], send.at[S_DT])
    wait_for(states.at[pl.ds(0, NG - 1)], send.at[S_ST])
    wait_for(qbuf.at[pl.ds(0, TOK)], send.at[S_Q])
    wait_for(newbuf.at[0], send.at[S_NK])
    wait_for(bcbuf.at[0, 0, pl.ds(0, NZ - 1)], send.at[S_BC])
    for pages in held[0] + held[1]:
        wait_for(pages, send.at[S_PG])
    wait_for(bcbuf.at[pl.ds(0, NX - 1), 0], send.at[S_BX])
    wait_for(bcbuf.at[:, 0], send.at[S_CORE])
    wait_for(obuf.at[pl.ds(0, TOK)], send.at[S_OUT])
    wait_for(stage.at[pl.ds(0, 7)], send.at[S_KV])
    wait_for(stage.at[0, 0], send.at[S_KV])
    wait_for(stage.at[0, 0, 0], send.at[S_KV])


def on_device(
    x_rows,
    dt_rows,
    bc_rows,
    a_log,
    d_skip,
    state_pool,
    owners,
    queries,
    new_kv,
    page_pool,
    page_table,
    prefix_len,
):
    me = lax.axis_index("dev")
    pages_here = page_pool.shape[0]
    holder, place = page_table // pages_here, page_table % pages_here
    x, z, c = me // (NZ * NC), (me // NC) % NZ, me % NC
    line = (x * NZ + jnp.arange(NZ, dtype=jnp.int32)) * NC + c
    slots = jnp.sum(
        jnp.where(holder[:, None, :] == line[None, :, None], place[:, None, :], 0), axis=2
    ).reshape(REQ * NZ)
    my_holder = lax.dynamic_index_in_dim(holder, me // NC, 0, keepdims=False)
    entry = jnp.arange(NDEV, dtype=jnp.int32)
    block = entry.reshape(NX, NZ, NC).transpose(0, 2, 1).reshape(NDEV)
    at = jnp.sum(jnp.where(my_holder[None, :] == block[:, None], entry[None, :], 0), axis=1)
    position = at[:, None] * PAGE + jnp.arange(PAGE, dtype=jnp.int32)[None, :]
    my_len = lax.dynamic_index_in_dim(prefix_len, me // NC, 0, keepdims=False)
    bias = jnp.where(position < my_len, 0.0, HIDDEN).astype(F32).reshape(1, PREFIX)
    dt_sent = dt_rows.astype(F32).T.reshape(NDEV, 2, TOK)
    smem = pl.BlockSpec(memory_space=pltpu.SMEM)
    vmem = pl.BlockSpec(memory_space=pltpu.VMEM)
    hbm = pl.BlockSpec(memory_space=pl.ANY)
    dma = pltpu.SemaphoreType.DMA
    ssd_out, finals, attn_out = pl.pallas_call(
        kernel,
        out_shape=(
            jax.ShapeDtypeStruct((REQ * NEW, 128), BF16),
            jax.ShapeDtypeStruct((REQ, 128, 128), F32),
            jax.ShapeDtypeStruct((TOK, 2 * QHALF), BF16),
        ),
        in_specs=[smem] * 4 + [vmem, hbm, hbm, hbm, vmem, hbm, hbm, hbm],
        out_specs=(hbm, hbm, hbm),
        scratch_shapes=[
            pltpu.VMEM((NZ, NX, NC, TOK, 128), BF16),
            pltpu.VMEM((NZ, NX, NC, 2, TOK), F32),
            pltpu.VMEM((NX, NC, NZ, TOK, 256), BF16),
            pltpu.VMEM((NG, 16, 128, 128), BF16),
            *[pltpu.VMEM((HELD, PAGE, 4 * HALF), BF16)] * 5,
            pltpu.VMEM((ROUTES, NX, NC, HEADS_CORE, 2, PAGE, 128), BF16),
            pltpu.VMEM((HEADS_CORE, 2, NX, NC, NZ, PAGE, 128), BF16),
            pltpu.VMEM((NEW, QHALF), BF16),
            pltpu.VMEM((2, NEW, HALF), BF16),
            pltpu.VMEM((NEW, QHALF), BF16),
            pltpu.VMEM((REQ, 8, NEW), F32),
            pltpu.VMEM((2 * REQ, NEW), F32),
            pltpu.VMEM((REQ * NEW, 128), BF16),
            pltpu.VMEM((REQ, 128, 128), F32),
            dma((8,)),
            dma((11,)),
            dma((2, 4)),
            dma((2, 2, PARTS)),
            dma((NZ,)),
            dma((NX,)),
            dma((NX,)),
            dma((2,)),
        ],
        compiler_params=pltpu.CompilerParams(
            collective_id=0, has_side_effects=True, vmem_limit_bytes=56 * 1024 * 1024
        ),
    )(
        slots,
        owners,
        a_log,
        d_skip,
        bias,
        dt_sent,
        x_rows,
        bc_rows,
        state_pool.reshape(16, 128, 128),
        queries,
        new_kv,
        page_pool,
    )
    return ssd_out, finals.reshape(REQ, 2, 64, 128), attn_out


def solution(mesh):
    return jax.shard_map(
        on_device,
        mesh=mesh,
        in_specs=(
            P(("grp", "dev"), None),
            P(("grp", "dev"), None),
            P(("grp", "dev"), None),
            P("dev"),
            P("dev"),
            P("grp", "dev", None, None),
            P("grp"),
            P(("grp", "dev"), None),
            P(("grp", "dev"), None),
            P(("grp", "dev"), None, None),
            P("grp", None),
            P("grp"),
        ),
        out_specs=(P("grp", "dev"), P("grp", "dev", None, None), P(("grp", "dev"), None)),
        check_vma=False,
    )
```

```python
import math

import jax
import jax.numpy as jnp
from jax import lax
from jax.experimental import pallas as pl
from jax.experimental.pallas import tpu as pltpu
from jax.sharding import PartitionSpec as P

MESH = pl.DeviceIdType.MESH
F32, BF16 = jnp.float32, jnp.bfloat16
NX, NZ, NC, NG = 4, 8, 2, 4
NDEV = NX * NZ * NC
REQ = 32
TOK = 128
NEW = 2 * TOK
HEADS_CORE = 4
QPER = 4
PAGE = 16
HELD = 8
PARTS = 2
ROUTES = 9
PIECES = 4
PREFIX = 1024
HALF = HEADS_CORE * 128
QHALF = HEADS_CORE * QPER * 128
PHASES = 2
PER_PHASE = HEADS_CORE // PHASES
LOG2E = math.log2(math.e)
EXP2_SCALE = LOG2E / math.sqrt(128.0)
HIDDEN = -1e30

NT = (((1,), (1,)), ((), ()))
TN = (((0,), (0,)), ((), ()))


def dot(a, b, dims=(((1,), (0,)), ((), ())), precision=None):
    return lax.dot_general(a, b, dims, precision=precision, preferred_element_type=F32)


def kernel(
    owners,
    a_log,
    d_skip,
    prefix_len,
    table_in,
    dt_in,
    x_in,
    bc_in,
    pool_in,
    q_in,
    kv_in,
    pages_in,
    ssd_hbm,
    fin_hbm,
    attn_hbm,
    xbuf,
    dtbuf,
    bcbuf,
    states,
    pool_own,
    up_near,
    up_far,
    down_near,
    down_far,
    stage,
    kvbuf,
    qbuf,
    newbuf,
    obuf,
    by_req,
    dt_rows,
    dt_stage,
    slots_v,
    slots,
    bias,
    ssd_v,
    fin_v,
    recv,
    send,
    ring_bc,
    ring_pg,
    recv_x,
    recv_bx,
    recv_c,
    out_sem,
):
    grp = lax.axis_index("grp")
    me = lax.axis_index("dev")
    myx, myz, myc = lax.div(me, NZ * NC), lax.rem(lax.div(me, NC), NZ), lax.rem(me, NC)
    other = me + 1 - 2 * myc

    def peer(step):
        x = lax.rem(myx + lax.div(step, NZ * NC), NX)
        z = lax.rem(myz + lax.div(step, NC), NZ)
        return (x * NZ + z) * NC + lax.rem(myc + step, NC)

    def remote(src, dst, send_sem, recv_sem, where):
        return pltpu.make_async_remote_copy(
            src_ref=src,
            dst_ref=dst,
            send_sem=send_sem,
            recv_sem=recv_sem,
            device_id=where,
            device_id_type=MESH,
        )

    def wait_for(ref, sem):
        pltpu.make_async_copy(ref, ref, sem).wait()

    R_DT, R_ST, R_Q, R_NK, R_BC, R_PG, R_KV, R_OUT = range(8)
    S_X, S_DT, S_ST, S_Q, S_NK, S_BC, S_PG, S_BX, S_KV, S_CORE, S_OUT = range(11)

    barrier = pltpu.get_barrier_semaphore()

    @pl.loop(1, NDEV)
    def _(step):
        pl.semaphore_signal(barrier, inc=1, device_id={"dev": peer(step)}, device_id_type=MESH)

    for dg in range(1, NG):
        pl.semaphore_signal(
            barrier, inc=1, device_id={"grp": (grp + dg) % NG}, device_id_type=MESH
        )

    holder, place = lax.shift_right_logical(table_in[...], 3), table_in[...] & (HELD - 1)
    lane = lax.broadcasted_iota(jnp.int32, (REQ, 128), 1)
    found = jnp.zeros((REQ, 128), jnp.int32)
    for z in range(NZ):
        line = (myx * NZ + z) * NC + myc
        here = jnp.sum(jnp.where(holder == line, place, 0), axis=1, keepdims=True)
        found = jnp.where(lane == z, here, found)
    slots_v[...] = found
    to_smem = pltpu.make_async_copy(slots_v, slots, out_sem.at[2])
    to_smem.start()

    by_head = dt_in[...].astype(F32).T
    for pair in range(NDEV):
        dt_stage[pair] = by_head[2 * pair : 2 * pair + 2]
    states[grp] = pool_in[...].astype(BF16)

    pl.semaphore_wait(barrier, NDEV - 1 + NG - 1)

    for dg in range(1, NG):
        remote(
            states.at[grp],
            states.at[grp],
            send.at[S_ST],
            recv.at[R_ST],
            {"grp": lax.rem(grp + dg, NG)},
        ).start()

    def on_ring(dz):
        return lax.rem(myz + dz + NZ, NZ)

    def at(x, z, c):
        return {"dev": (x * NZ + z) * NC + c}

    def map_rows(side):
        return pl.ds(side * (TOK // 2), TOK // 2)

    def page_rows(part):
        return pl.ds(part * (HELD // PARTS), HELD // PARTS)

    ways = (1, -1)
    held = ((up_near, up_far), (down_near, down_far))

    def pass_maps(step, side, source, distance=1, rows=None):
        block = bcbuf.at[myx, myc, on_ring(-min(step - 1, 2) * ways[side])]
        if rows is not None:
            block = block.at[rows]
        remote(
            block if source is None else source,
            block,
            send.at[S_BC],
            ring_bc.at[side, step - 1],
            at(myx, on_ring(distance * ways[side]), myc),
        ).start()

    def pass_pages(step, side, part):
        source = pages_in if step == 1 else held[side][0]
        remote(
            source.at[page_rows(part)],
            held[side][step - 1].at[page_rows(part)],
            send.at[S_PG],
            ring_pg.at[side, step - 1, part],
            at(myx, on_ring(ways[side]), myc),
        ).start()

    for side in range(2):
        pass_maps(1, side, bc_in)
    for part in range(PARTS):
        for side in range(2):
            pass_pages(1, side, part)
    own_pages = pltpu.make_async_copy(pages_in, pool_own, recv.at[R_PG])
    own_pages.start()
    own_maps = pltpu.make_async_copy(bc_in, bcbuf.at[myx, myc, myz], recv.at[R_BC])
    own_maps.start()

    def send_x(dz, k):
        x = lax.rem(myx + lax.div(k, NC), NX)
        to = (x * NZ + lax.rem(myz + dz, NZ)) * NC + lax.rem(myc + k, NC)
        remote(
            x_in.at[:, pl.ds(pl.multiple_of(to * 128, 128), 128)],
            xbuf.at[myz, myx, myc],
            send.at[S_X],
            recv_x.at[dz],
            {"dev": to},
        ).start()

    pltpu.make_async_copy(
        x_in.at[:, pl.ds(pl.multiple_of(me * 128, 128), 128)],
        xbuf.at[myz, myx, myc],
        recv_x.at[0],
    ).start()
    pltpu.make_async_copy(dt_stage.at[me], dtbuf.at[myz, myx, myc], recv.at[R_DT]).start()

    @pl.loop(1, NX * NC)
    def _(k):
        send_x(0, k)

    @pl.loop(1, NDEV)
    def _(step):
        to = peer(step)
        remote(
            dt_stage.at[to], dtbuf.at[myz, myx, myc], send.at[S_DT], recv.at[R_DT], {"dev": to}
        ).start()

    def send_both_ways(near):
        @pl.loop(0, 2 * NX * NC)
        def _(i):
            send_x(near + lax.rem(i, 2) * (NZ - 2 * near), lax.div(i, 2))

    def send_far():
        @pl.loop(0, NX * NC)
        def _(k):
            send_x(4, k)

    my_rows = pl.ds(pl.multiple_of(myc * TOK, TOK), TOK)

    def half(ref, start, width, core):
        return ref.at[:, pl.ds(pl.multiple_of(start + core * width, width), width)]

    pltpu.make_async_copy(half(q_in, 0, QHALF, myc), qbuf.at[my_rows], recv.at[R_Q]).start()
    remote(
        half(q_in, 0, QHALF, 1 - myc),
        qbuf.at[my_rows],
        send.at[S_Q],
        recv.at[R_Q],
        {"dev": other},
    ).start()
    for kv in range(2):
        pltpu.make_async_copy(
            half(kv_in, kv * 2 * HALF, HALF, myc), newbuf.at[kv, my_rows], recv.at[R_NK]
        ).start()
        remote(
            half(kv_in, kv * 2 * HALF, HALF, 1 - myc),
            newbuf.at[kv, my_rows],
            send.at[S_NK],
            recv.at[R_NK],
            {"dev": other},
        ).start()

    def spread_maps(z):
        block = bcbuf.at[myx, myc, z]
        for dx in range(1, NX):
            remote(
                block,
                block,
                send.at[S_BX],
                recv_bx.at[dx],
                at(lax.rem(myx + dx, NX), myz, myc),
            ).start()

    def spread_pages(place, pages, away, onward=0, cores=(0, 1)):
        z, target = on_ring(away), on_ring(onward)
        mine = kvbuf.at[:, :, myx, myc, z]

        @pl.loop(0, NX)
        def _(x):
            slot = slots[x * NZ + target, z]
            for kv in range(2):
                for c in cores:
                    for hh in range(HEADS_CORE):
                        col = ((kv * 2 + c) * HEADS_CORE + hh) * 128
                        stage[place, x, c, hh, kv] = pages[slot, :, col : col + 128]

        def pages_to(x, c):
            remote(
                stage.at[place, x, c], mine, send.at[S_KV], recv.at[R_KV], at(x, target, c)
            ).start()

        if onward == 0:
            pltpu.make_async_copy(stage.at[place, myx, myc], mine, recv.at[R_KV]).start()

            @pl.loop(1, NX * NC)
            def _(k):
                pages_to(lax.rem(myx + lax.div(k, NC), NX), lax.rem(myc + k, NC))
        elif len(cores) == 2:

            @pl.loop(0, NX * NC)
            def _(k):
                pages_to(lax.rem(myx + lax.div(k, NC), NX), lax.rem(myc + k, NC))
        else:

            @pl.loop(0, NX)
            def _(dx):
                pages_to(lax.rem(myx + dx, NX), cores[0])

    mine = lax.broadcasted_iota(jnp.int32, (REQ, NDEV), 0) == lax.div(me, NC)
    my_holders = jnp.sum(jnp.where(mine, holder.astype(F32), 0.0), axis=0, keepdims=True)
    block = lax.broadcasted_iota(jnp.int32, (NDEV, NDEV), 0)
    block_holder = (
        (block // (NC * NZ)) * (NC * NZ) + (block % NZ) * NC + (block // NZ) % NC
    ).astype(F32)
    entry = lax.broadcasted_iota(jnp.int32, (8, NDEV), 1).astype(F32)
    found_at = dot(entry, (my_holders == block_holder).astype(F32), NT)
    key = lax.broadcasted_iota(jnp.int32, (NDEV, PREFIX), 1)
    spread = (key // PAGE == lax.broadcasted_iota(jnp.int32, (NDEV, PREFIX), 0)).astype(F32)
    position = dot(found_at, spread) * PAGE + (
        lax.broadcasted_iota(jnp.int32, (8, PREFIX), 1) % PAGE
    ).astype(F32)
    length = jnp.full((8, PREFIX), prefix_len[lax.div(me, NC)]).astype(F32)
    bias[...] = jnp.where(position < length, 0.0, HIDDEN)

    to_smem.wait()
    own_maps.wait()
    spread_maps(myz)
    own_pages.wait()
    spread_pages(0, pool_own, 0)
    for step in (1, 2):
        for side in range(2):
            z = on_ring(-step * ways[side])
            wait_for(bcbuf.at[myx, myc, z], ring_bc.at[side, step - 1])
            pass_maps(step + 1, side, None)
            if step == 2:
                pass_maps(4, side, None, 2, map_rows(side))
        for part in range(PARTS):
            for side in range(2):
                wait_for(
                    held[side][step - 1].at[page_rows(part)], ring_pg.at[side, step - 1, part]
                )
                if step == 1:
                    pass_pages(2, side, part)
        for side in range(2):
            spread_maps(on_ring(-step * ways[side]))
        if step == 2:
            for side in range(2):
                spread_pages(5 + side, held[side][1], -2 * ways[side], 2 * ways[side], (side,))
            for side in range(2):
                spread_pages(7 + side, held[side][1], -2 * ways[side], ways[side])
        for side in range(2):
            spread_pages(2 * step - 1 + side, held[side][step - 1], -step * ways[side])

    for side in range(2):
        z = on_ring(-3 * ways[side])
        wait_for(bcbuf.at[myx, myc, z], ring_bc.at[side, 2])
        spread_maps(z)
    far = on_ring(4)
    for side in range(2):
        wait_for(bcbuf.at[myx, myc, far, map_rows(side)], ring_bc.at[side, 3])
    spread_maps(far)
    send_far()
    send_both_ways(3)

    def maps_to_other_core():
        for dx in range(NX):
            block = bcbuf.at[lax.rem(myx + NX - dx, NX), myc]
            if dx:
                wait_for(block, recv_bx.at[dx])
            remote(block, block, send.at[S_CORE], recv_c.at[dx], {"dev": other}).start()

    maps_to_other_core()
    send_both_ways(2)
    send_both_ways(1)
    wait_for(qbuf, recv.at[R_Q])
    wait_for(newbuf, recv.at[R_NK])
    wait_for(kvbuf, recv.at[R_KV])
    causal = lax.broadcasted_iota(jnp.int32, (NEW, NEW), 0) >= lax.broadcasted_iota(
        jnp.int32, (NEW, NEW), 1
    )
    for p in range(PHASES):
        @pl.loop(p * PER_PHASE * QPER, (p + 1) * PER_PHASE * QPER)
        def _(qh):
            h = lax.div(qh, QPER)
            head_cols = pl.ds(pl.multiple_of(h * 128, 128), 128)
            q = qbuf[:, pl.ds(pl.multiple_of(qh * 128, 128), 128)]
            keys = kvbuf[h, 0].reshape(PREFIX, 128)
            values = kvbuf[h, 1].reshape(PREFIX, 128)
            old = dot(q, keys, NT) + bias[0:1, :]
            new = jnp.where(causal, dot(q, newbuf[0, :, head_cols], NT), HIDDEN)
            top = jnp.maximum(
                jnp.max(old, axis=1, keepdims=True), jnp.max(new, axis=1, keepdims=True)
            )
            shift = top * EXP2_SCALE
            old = jnp.exp2(old * EXP2_SCALE - shift)
            new = jnp.exp2(new * EXP2_SCALE - shift)
            totals = jnp.sum(old, axis=1, keepdims=True) + jnp.sum(new, axis=1, keepdims=True)
            mixed = dot(old.astype(BF16), values) + dot(
                new.astype(BF16), newbuf[1, :, head_cols]
            )
            obuf[:, pl.ds(pl.multiple_of(qh * 128, 128), 128)] = (mixed / totals).astype(BF16)

        width = QHALF // PHASES
        src_cols = pl.ds(p * width, width)
        dst_cols = pl.ds(pl.multiple_of(myc * QHALF + p * width, width), width)
        pltpu.make_async_copy(
            obuf.at[my_rows, src_cols], attn_hbm.at[:, dst_cols], recv.at[R_OUT]
        ).start()
        remote(
            obuf.at[pl.ds(pl.multiple_of((1 - myc) * TOK, TOK), TOK), src_cols],
            attn_hbm.at[:, dst_cols],
            send.at[S_OUT],
            recv.at[R_OUT],
            {"dev": other},
        ).start()

    wait_for(dtbuf, recv.at[R_DT])
    wait_for(states.at[pl.ds(0, NG - 1)], recv.at[R_ST])
    for dx in range(NX):
        wait_for(bcbuf.at[lax.rem(myx + NX - dx, NX), 1 - myc], recv_c.at[dx])

    for r in range(REQ):
        for c in range(NC):
            dt_rows[2 * r : 2 * r + 2, c * TOK : (c + 1) * TOK] = dtbuf[r % NZ, r // NZ, c]
    odd_row = lax.broadcasted_iota(jnp.int32, (2 * REQ, NEW), 0) % 2 == 1
    rate = -jnp.exp(
        jnp.where(odd_row, jnp.full((2 * REQ, NEW), a_log[1]), jnp.full((2 * REQ, NEW), a_log[0]))
    )
    earlier = lax.broadcasted_iota(jnp.int32, (NEW, NEW), 0)
    later = lax.broadcasted_iota(jnp.int32, (NEW, NEW), 1)
    cumulative = dot(
        dt_rows[...] * (rate * LOG2E),
        (earlier <= later).astype(F32),
        precision=lax.Precision.HIGHEST,
    )
    less_step = cumulative - jnp.log2(dt_rows[...])
    for r in range(REQ):
        by_req[r, 0:2, :] = cumulative[2 * r : 2 * r + 2]
        by_req[r, 2:4, :] = less_step[2 * r : 2 * r + 2]

    second = lax.broadcasted_iota(jnp.int32, (1, 128), 1) >= 64
    skip = jnp.where(second, jnp.full((1, 128), d_skip[1]), jnp.full((1, 128), d_skip[0]))
    keep_second = second.astype(F32).astype(BF16)
    keep_first = (1.0 - second.astype(F32)).astype(BF16)
    low_half = lax.broadcasted_iota(jnp.int32, (128, 1), 0) < 64
    term = lax.broadcasted_iota(jnp.int32, (32, 4 * TOK), 0)
    lane = lax.broadcasted_iota(jnp.int32, (32, 4 * TOK), 1)
    wanted = jnp.where(lane < 2 * TOK, lane // TOK, 2 + lane // 64 - 4)
    chosen = ((term % 8 == wanted) & (term < 24)).astype(F32).astype(BF16)
    diagonal = lax.broadcasted_iota(jnp.int32, (TOK, TOK), 0) >= lax.broadcasted_iota(
        jnp.int32, (TOK, TOK), 1
    )

    def ssd_request(rx, rz):
        r = rx * NZ + rz
        x = jnp.concatenate([xbuf[rz, rx, 0], xbuf[rz, rx, 1]], axis=0)
        bc = jnp.concatenate([bcbuf[rx, 0, rz], bcbuf[rx, 1, rz]], axis=0)
        b, c = bc[:, :128], bc[:, 128:]
        kept = states[lax.div(owners[r], 16), lax.rem(owners[r], 16)]
        cum = by_req[r, 0:2, :]
        shifted = by_req[r, 2:4, :]
        last = cum[:, NEW - 1 :]
        rows = jnp.concatenate([cum, jnp.exp2(cum), jnp.exp2(last - shifted), cum], axis=0)
        high = rows.astype(BF16)
        left_over = rows - high.astype(F32)
        middle = left_over.astype(BF16)
        low = (left_over - middle.astype(F32)).astype(BF16)
        wide = dot(jnp.concatenate([high, middle, low, low], axis=0), chosen, TN)
        growth, gain = wide[:, 2 * TOK : 3 * TOK], wide[:, 3 * TOK :]
        inner_first = dot(c[:TOK], b[:TOK], NT)
        inner_second = dot(c[TOK:], b, NT)

        def decayed(h, inner, i, j):
            diff = (
                wide[i * TOK : (i + 1) * TOK, h * TOK : (h + 1) * TOK]
                - shifted[h : h + 1, j * TOK : (j + 1) * TOK]
            )
            if i == j:
                diff = jnp.where(diagonal, diff, HIDDEN)
            return (jnp.exp2(diff) * inner).astype(BF16)

        upper, lower = [], []
        for h in range(2):
            upper.append(decayed(h, inner_first, 0, 0))
            lower.append(decayed(h, inner_second[:, :TOK], 1, 0))
            lower.append(decayed(h, inner_second[:, TOK:], 1, 1))
        x_first = x * keep_first
        x_second = x * keep_second
        within = jnp.concatenate(
            [
                dot(
                    jnp.concatenate(upper, axis=1),
                    jnp.concatenate([x_first[:TOK], x_second[:TOK]], axis=0),
                ),
                dot(
                    jnp.concatenate(lower, axis=1), jnp.concatenate([x_first, x_second], axis=0)
                ),
            ],
            axis=0,
        )
        x_float = x.astype(F32)
        carried = growth * dot(c, kept, NT)
        ssd_v[pl.ds(pl.multiple_of(r * NEW, NEW), NEW), :] = (
            within + carried + skip * x_float
        ).astype(BF16)
        weighted = (x_float * gain).astype(BF16)
        total = jnp.exp2(last)
        left = jnp.where(
            low_half,
            jnp.broadcast_to(total[0:1], (128, 1)),
            jnp.broadcast_to(total[1:2], (128, 1)),
        )
        fin_v[r] = dot(weighted, b, TN) + left * kept.astype(F32)

    @pl.loop(0, NZ)
    def _(i):
        j = lax.rem(i + NZ - 1, NZ)
        odd = lax.rem(j, 2)
        dz = 4 + (1 - odd) * lax.div(j, 2) - odd * lax.div(j + 1, 2)
        rz = lax.rem(myz + NZ - dz, NZ)
        wait_for(xbuf.at[rz], recv_x.at[dz])

        for rx in range(NX):
            ssd_request(rx, rz)
        for rx in range(NX):
            r = rx * NZ + rz
            rows = pl.ds(pl.multiple_of(r * NEW, NEW), NEW)
            pltpu.make_async_copy(ssd_v.at[rows], ssd_hbm.at[rows], out_sem.at[0]).start()
            pltpu.make_async_copy(fin_v.at[r], fin_hbm.at[r], out_sem.at[1]).start()

    wait_for(ssd_v, out_sem.at[0])
    wait_for(fin_v, out_sem.at[1])
    wait_for(attn_hbm, recv.at[R_OUT])
    wait_for(xbuf.at[pl.ds(0, NZ - 1)], send.at[S_X])
    wait_for(xbuf.at[0, pl.ds(0, NX - 1)], send.at[S_X])
    wait_for(xbuf.at[0, 0, 0], send.at[S_X])
    wait_for(dtbuf.at[pl.ds(0, NZ - 1)], send.at[S_DT])
    wait_for(dtbuf.at[0, pl.ds(0, NX - 1)], send.at[S_DT])
    wait_for(dtbuf.at[0, 0, 0], send.at[S_DT])
    wait_for(states.at[pl.ds(0, NG - 1)], send.at[S_ST])
    wait_for(qbuf.at[pl.ds(0, TOK)], send.at[S_Q])
    wait_for(newbuf.at[0], send.at[S_NK])
    wait_for(bcbuf.at[0, 0, pl.ds(0, NZ - 1)], send.at[S_BC])
    for pages in held[0] + held[1]:
        wait_for(pages, send.at[S_PG])
    wait_for(bcbuf.at[pl.ds(0, NX - 1), 0], send.at[S_BX])
    wait_for(bcbuf.at[:, 0], send.at[S_CORE])
    wait_for(obuf.at[pl.ds(0, TOK)], send.at[S_OUT])
    wait_for(stage.at[pl.ds(0, 7)], send.at[S_KV])
    wait_for(stage.at[0, 0], send.at[S_KV])
    wait_for(stage.at[0, 0, 0], send.at[S_KV])


def hand_over(*refs):
    sources, targets, held, (arrived, left) = refs[:3], refs[3:6], refs[6:9], refs[9:]

    def piece(ref, part):
        rows = ref.shape[0] // PIECES
        return ref.at[pl.ds(part * rows, rows)]

    for part in range(PIECES):
        for i in range(3):
            pltpu.make_async_copy(
                piece(sources[i], part), piece(held[i], part), arrived.at[i, part]
            ).start()
    for part in range(PIECES):
        for i in range(3):
            pltpu.make_async_copy(
                piece(sources[i], part), piece(held[i], part), arrived.at[i, part]
            ).wait()
            pltpu.make_async_copy(piece(held[i], part), piece(targets[i], part), left.at[i]).start()
    for i in range(3):
        pltpu.make_async_copy(held[i], targets[i], left.at[i]).wait()


def on_device(
    x_rows,
    dt_rows,
    bc_rows,
    a_log,
    d_skip,
    state_pool,
    owners,
    queries,
    new_kv,
    page_pool,
    page_table,
    prefix_len,
):
    smem = pl.BlockSpec(memory_space=pltpu.SMEM)
    vmem = pl.BlockSpec(memory_space=pltpu.VMEM)
    hbm = pl.BlockSpec(memory_space=pl.ANY)
    dma = pltpu.SemaphoreType.DMA
    ssd_out, finals, attn_out = pl.pallas_call(
        kernel,
        out_shape=(
            jax.ShapeDtypeStruct((REQ * NEW, 128), BF16),
            jax.ShapeDtypeStruct((REQ, 128, 128), F32),
            jax.ShapeDtypeStruct((TOK, 2 * QHALF), BF16),
        ),
        in_specs=[smem] * 4 + [vmem, vmem, hbm, hbm, vmem, hbm, hbm, hbm],
        out_specs=(hbm, hbm, hbm),
        scratch_shapes=[
            pltpu.VMEM((NZ, NX, NC, TOK, 128), BF16),
            pltpu.VMEM((NZ, NX, NC, 2, TOK), F32),
            pltpu.VMEM((NX, NC, NZ, TOK, 256), BF16),
            pltpu.VMEM((NG, 16, 128, 128), BF16),
            *[pltpu.VMEM((HELD, PAGE, 4 * HALF), BF16)] * 5,
            pltpu.VMEM((ROUTES, NX, NC, HEADS_CORE, 2, PAGE, 128), BF16),
            pltpu.VMEM((HEADS_CORE, 2, NX, NC, NZ, PAGE, 128), BF16),
            pltpu.VMEM((NEW, QHALF), BF16),
            pltpu.VMEM((2, NEW, HALF), BF16),
            pltpu.VMEM((NEW, QHALF), BF16),
            pltpu.VMEM((REQ, 8, NEW), F32),
            pltpu.VMEM((2 * REQ, NEW), F32),
            pltpu.VMEM((NDEV, 2, TOK), F32),
            pltpu.VMEM((REQ, 128), jnp.int32),
            pltpu.SMEM((REQ, 128), jnp.int32),
            pltpu.VMEM((8, PREFIX), F32),
            pltpu.VMEM((REQ * NEW, 128), BF16),
            pltpu.VMEM((REQ, 128, 128), F32),
            dma((8,)),
            dma((11,)),
            dma((2, 4)),
            dma((2, 2, PARTS)),
            dma((NZ,)),
            dma((NX,)),
            dma((NX,)),
            dma((3,)),
        ],
        compiler_params=pltpu.CompilerParams(
            collective_id=0, has_side_effects=True, vmem_limit_bytes=56 * 1024 * 1024
        ),
    )(
        owners,
        a_log,
        d_skip,
        prefix_len,
        page_table,
        dt_rows,
        x_rows,
        bc_rows,
        state_pool.reshape(16, 128, 128),
        queries,
        new_kv,
        page_pool,
    )
    outs = (ssd_out, finals, attn_out)
    ssd_out, finals, attn_out = pl.pallas_call(
        hand_over,
        out_shape=tuple(jax.ShapeDtypeStruct(a.shape, a.dtype) for a in outs),
        in_specs=[hbm] * 3,
        out_specs=(hbm,) * 3,
        scratch_shapes=[pltpu.VMEM(a.shape, a.dtype) for a in outs] + [dma((3, PIECES)), dma((3,))],
        compiler_params=pltpu.CompilerParams(vmem_limit_bytes=60 * 1024 * 1024),
    )(*outs)
    return ssd_out, finals.reshape(REQ, 2, 64, 128), attn_out


def solution(mesh):
    return jax.shard_map(
        on_device,
        mesh=mesh,
        in_specs=(
            P(("grp", "dev"), None),
            P(("grp", "dev"), None),
            P(("grp", "dev"), None),
            P("dev"),
            P("dev"),
            P("grp", "dev", None, None),
            P("grp"),
            P(("grp", "dev"), None),
            P(("grp", "dev"), None),
            P(("grp", "dev"), None, None),
            P("grp", None),
            P("grp"),
        ),
        out_specs=(P("grp", "dev"), P("grp", "dev", None, None), P(("grp", "dev"), None)),
        check_vma=False,
    )
```

```python
import math

import jax
import jax.numpy as jnp
from jax import lax
from jax.experimental import pallas as pl
from jax.experimental.pallas import tpu as pltpu
from jax.sharding import PartitionSpec as P

MESH = pl.DeviceIdType.MESH
F32, BF16 = jnp.float32, jnp.bfloat16
NX, NZ, NC, NG = 4, 8, 2, 4
NDEV = NX * NZ * NC
REQ = 32
TOK = 128
NEW = 2 * TOK
HEADS_CORE = 4
QPER = 4
PAGE = 16
HELD = 8
PARTS = 1
ROUTES = 9
PIECES = 4
PREFIX = 1024
HALF = HEADS_CORE * 128
QHALF = HEADS_CORE * QPER * 128
PHASES = 2
PER_PHASE = HEADS_CORE // PHASES
LOG2E = math.log2(math.e)
EXP2_SCALE = LOG2E / math.sqrt(128.0)
HIDDEN = -1e30

NT = (((1,), (1,)), ((), ()))
TN = (((0,), (0,)), ((), ()))


def dot(a, b, dims=(((1,), (0,)), ((), ())), precision=None):
    return lax.dot_general(a, b, dims, precision=precision, preferred_element_type=F32)


def kernel(
    owners,
    a_log,
    d_skip,
    prefix_len,
    table_in,
    dt_in,
    x_in,
    bc_in,
    pool_in,
    q_in,
    kv_in,
    pages_in,
    ssd_v,
    fin_v,
    attn_v,
    xbuf,
    dtbuf,
    bcbuf,
    states,
    pool_own,
    up_near,
    up_far,
    down_near,
    down_far,
    stage,
    kvbuf,
    qbuf,
    newbuf,
    obuf,
    by_req,
    dt_rows,
    dt_stage,
    slots_v,
    slots,
    bias,
    recv,
    send,
    ring_bc,
    ring_pg,
    recv_x,
    recv_bx,
    recv_c,
    out_sem,
):
    grp = lax.axis_index("grp")
    me = lax.axis_index("dev")
    myx, myz, myc = lax.div(me, NZ * NC), lax.rem(lax.div(me, NC), NZ), lax.rem(me, NC)
    other = me + 1 - 2 * myc

    def peer(step):
        x = lax.rem(myx + lax.div(step, NZ * NC), NX)
        z = lax.rem(myz + lax.div(step, NC), NZ)
        return (x * NZ + z) * NC + lax.rem(myc + step, NC)

    def remote(src, dst, send_sem, recv_sem, where):
        return pltpu.make_async_remote_copy(
            src_ref=src,
            dst_ref=dst,
            send_sem=send_sem,
            recv_sem=recv_sem,
            device_id=where,
            device_id_type=MESH,
        )

    def wait_for(ref, sem):
        pltpu.make_async_copy(ref, ref, sem).wait()

    R_DT, R_ST, R_Q, R_NK, R_BC, R_PG, R_KV, R_OUT = range(8)
    S_X, S_DT, S_ST, S_Q, S_NK, S_BC, S_PG, S_BX, S_KV, S_CORE, S_OUT = range(11)

    barrier = pltpu.get_barrier_semaphore()

    @pl.loop(1, NDEV)
    def _(step):
        pl.semaphore_signal(barrier, inc=1, device_id={"dev": peer(step)}, device_id_type=MESH)

    for dg in range(1, NG):
        pl.semaphore_signal(
            barrier, inc=1, device_id={"grp": (grp + dg) % NG}, device_id_type=MESH
        )

    pl.semaphore_wait(barrier, NDEV - 1 + NG - 1)

    def on_ring(dz):
        return lax.rem(myz + dz + NZ, NZ)

    def at(x, z, c):
        return {"dev": (x * NZ + z) * NC + c}

    def map_rows(side):
        return pl.ds(side * (TOK // 2), TOK // 2)

    def page_rows(part):
        return pl.ds(part * (HELD // PARTS), HELD // PARTS)

    ways = (1, -1)
    held = ((up_near, up_far), (down_near, down_far))

    def pass_maps(step, side, source, distance=1, rows=None):
        block = bcbuf.at[myx, myc, on_ring(-min(step - 1, 2) * ways[side])]
        if rows is not None:
            block = block.at[rows]
        remote(
            block if source is None else source,
            block,
            send.at[S_BC],
            ring_bc.at[side, step - 1],
            at(myx, on_ring(distance * ways[side]), myc),
        ).start()

    def pass_pages(step, side, part):
        source = pages_in if step == 1 else held[side][0]
        remote(
            source.at[page_rows(part)],
            held[side][step - 1].at[page_rows(part)],
            send.at[S_PG],
            ring_pg.at[side, step - 1, part],
            at(myx, on_ring(ways[side]), myc),
        ).start()

    for side in range(2):
        pass_maps(1, side, bc_in)
    for part in range(PARTS):
        for side in range(2):
            pass_pages(1, side, part)
    own_pages = pltpu.make_async_copy(pages_in, pool_own, recv.at[R_PG])
    own_pages.start()
    own_maps = pltpu.make_async_copy(bc_in, bcbuf.at[myx, myc, myz], recv.at[R_BC])
    own_maps.start()

    def send_x(dz, k):
        x = lax.rem(myx + lax.div(k, NC), NX)
        to = (x * NZ + lax.rem(myz + dz, NZ)) * NC + lax.rem(myc + k, NC)
        remote(
            x_in.at[:, pl.ds(pl.multiple_of(to * 128, 128), 128)],
            xbuf.at[myz, myx, myc],
            send.at[S_X],
            recv_x.at[dz],
            {"dev": to},
        ).start()

    pltpu.make_async_copy(
        x_in.at[:, pl.ds(pl.multiple_of(me * 128, 128), 128)],
        xbuf.at[myz, myx, myc],
        recv_x.at[0],
    ).start()

    @pl.loop(1, NX * NC)
    def _(k):
        send_x(0, k)

    holder, place = lax.shift_right_logical(table_in[...], 3), table_in[...] & (HELD - 1)
    lane = lax.broadcasted_iota(jnp.int32, (REQ, 128), 1)
    found = jnp.zeros((REQ, 128), jnp.int32)
    for z in range(NZ):
        line = (myx * NZ + z) * NC + myc
        here = jnp.sum(jnp.where(holder == line, place, 0), axis=1, keepdims=True)
        found = jnp.where(lane == z, here, found)
    slots_v[...] = found
    to_smem = pltpu.make_async_copy(slots_v, slots, out_sem.at[0])
    to_smem.start()

    by_head = dt_in[...].astype(F32).T
    for pair in range(NDEV):
        dt_stage[pair] = by_head[2 * pair : 2 * pair + 2]
    states[grp] = pool_in[...].astype(BF16)

    for dg in range(1, NG):
        remote(
            states.at[grp],
            states.at[grp],
            send.at[S_ST],
            recv.at[R_ST],
            {"grp": lax.rem(grp + dg, NG)},
        ).start()

    pltpu.make_async_copy(dt_stage.at[me], dtbuf.at[myz, myx, myc], recv.at[R_DT]).start()

    @pl.loop(1, NDEV)
    def _(step):
        to = peer(step)
        remote(
            dt_stage.at[to], dtbuf.at[myz, myx, myc], send.at[S_DT], recv.at[R_DT], {"dev": to}
        ).start()

    def send_both_ways(near):
        @pl.loop(0, 2 * NX * NC)
        def _(i):
            send_x(near + lax.rem(i, 2) * (NZ - 2 * near), lax.div(i, 2))

    def send_far():
        @pl.loop(0, NX * NC)
        def _(k):
            send_x(4, k)

    my_rows = pl.ds(pl.multiple_of(myc * TOK, TOK), TOK)

    def half(ref, start, width, core):
        return ref.at[:, pl.ds(pl.multiple_of(start + core * width, width), width)]

    pltpu.make_async_copy(half(q_in, 0, QHALF, myc), qbuf.at[my_rows], recv.at[R_Q]).start()
    remote(
        half(q_in, 0, QHALF, 1 - myc),
        qbuf.at[my_rows],
        send.at[S_Q],
        recv.at[R_Q],
        {"dev": other},
    ).start()
    for kv in range(2):
        pltpu.make_async_copy(
            half(kv_in, kv * 2 * HALF, HALF, myc), newbuf.at[kv, my_rows], recv.at[R_NK]
        ).start()
        remote(
            half(kv_in, kv * 2 * HALF, HALF, 1 - myc),
            newbuf.at[kv, my_rows],
            send.at[S_NK],
            recv.at[R_NK],
            {"dev": other},
        ).start()

    def spread_maps(z):
        block = bcbuf.at[myx, myc, z]
        for dx in range(1, NX):
            remote(
                block,
                block,
                send.at[S_BX],
                recv_bx.at[dx],
                at(lax.rem(myx + dx, NX), myz, myc),
            ).start()

    def spread_pages(place, pages, away, onward=0, cores=(0, 1)):
        z, target = on_ring(away), on_ring(onward)
        mine = kvbuf.at[:, :, myx, myc, z]

        @pl.loop(0, NX)
        def _(x):
            slot = slots[x * NZ + target, z]
            for kv in range(2):
                for c in cores:
                    for hh in range(HEADS_CORE):
                        col = ((kv * 2 + c) * HEADS_CORE + hh) * 128
                        stage[place, x, c, hh, kv] = pages[slot, :, col : col + 128]

        def pages_to(x, c):
            remote(
                stage.at[place, x, c], mine, send.at[S_KV], recv.at[R_KV], at(x, target, c)
            ).start()

        if onward == 0:
            pltpu.make_async_copy(stage.at[place, myx, myc], mine, recv.at[R_KV]).start()

            @pl.loop(1, NX * NC)
            def _(k):
                pages_to(lax.rem(myx + lax.div(k, NC), NX), lax.rem(myc + k, NC))
        elif len(cores) == 2:

            @pl.loop(0, NX * NC)
            def _(k):
                pages_to(lax.rem(myx + lax.div(k, NC), NX), lax.rem(myc + k, NC))
        else:

            @pl.loop(0, NX)
            def _(dx):
                pages_to(lax.rem(myx + dx, NX), cores[0])

    mine = lax.broadcasted_iota(jnp.int32, (REQ, NDEV), 0) == lax.div(me, NC)
    my_holders = jnp.sum(jnp.where(mine, holder.astype(F32), 0.0), axis=0, keepdims=True)
    block = lax.broadcasted_iota(jnp.int32, (NDEV, NDEV), 0)
    block_holder = (
        (block // (NC * NZ)) * (NC * NZ) + (block % NZ) * NC + (block // NZ) % NC
    ).astype(F32)
    entry = lax.broadcasted_iota(jnp.int32, (8, NDEV), 1).astype(F32)
    found_at = dot(entry, (my_holders == block_holder).astype(F32), NT)
    key = lax.broadcasted_iota(jnp.int32, (NDEV, PREFIX), 1)
    spread = (key // PAGE == lax.broadcasted_iota(jnp.int32, (NDEV, PREFIX), 0)).astype(F32)
    position = dot(found_at, spread) * PAGE + (
        lax.broadcasted_iota(jnp.int32, (8, PREFIX), 1) % PAGE
    ).astype(F32)
    length = jnp.full((8, PREFIX), prefix_len[lax.div(me, NC)]).astype(F32)
    bias[...] = jnp.where(position < length, 0.0, HIDDEN)

    to_smem.wait()
    own_maps.wait()
    spread_maps(myz)
    own_pages.wait()
    spread_pages(0, pool_own, 0)
    for step in (1, 2):
        for side in range(2):
            z = on_ring(-step * ways[side])
            wait_for(bcbuf.at[myx, myc, z], ring_bc.at[side, step - 1])
            pass_maps(step + 1, side, None)
            if step == 2:
                pass_maps(4, side, None, 2, map_rows(side))
        for part in range(PARTS):
            for side in range(2):
                wait_for(
                    held[side][step - 1].at[page_rows(part)], ring_pg.at[side, step - 1, part]
                )
                if step == 1:
                    pass_pages(2, side, part)
        for side in range(2):
            spread_maps(on_ring(-step * ways[side]))
        if step == 2:
            for side in range(2):
                spread_pages(5 + side, held[side][1], -2 * ways[side], 2 * ways[side], (side,))
            for side in range(2):
                spread_pages(7 + side, held[side][1], -2 * ways[side], ways[side])
        for side in range(2):
            spread_pages(2 * step - 1 + side, held[side][step - 1], -step * ways[side])

    for side in range(2):
        z = on_ring(-3 * ways[side])
        wait_for(bcbuf.at[myx, myc, z], ring_bc.at[side, 2])
        spread_maps(z)
    far = on_ring(4)
    for side in range(2):
        wait_for(bcbuf.at[myx, myc, far, map_rows(side)], ring_bc.at[side, 3])
    spread_maps(far)
    send_far()
    send_both_ways(3)

    def maps_to_other_core():
        for dx in range(NX):
            block = bcbuf.at[lax.rem(myx + NX - dx, NX), myc]
            if dx:
                wait_for(block, recv_bx.at[dx])
            remote(block, block, send.at[S_CORE], recv_c.at[dx], {"dev": other}).start()

    maps_to_other_core()
    send_both_ways(2)
    send_both_ways(1)
    wait_for(qbuf, recv.at[R_Q])
    wait_for(newbuf, recv.at[R_NK])
    wait_for(kvbuf, recv.at[R_KV])
    causal = lax.broadcasted_iota(jnp.int32, (NEW, NEW), 0) >= lax.broadcasted_iota(
        jnp.int32, (NEW, NEW), 1
    )
    for p in range(PHASES):
        @pl.loop(p * PER_PHASE * QPER, (p + 1) * PER_PHASE * QPER)
        def _(qh):
            h = lax.div(qh, QPER)
            head_cols = pl.ds(pl.multiple_of(h * 128, 128), 128)
            q = qbuf[:, pl.ds(pl.multiple_of(qh * 128, 128), 128)]
            keys = kvbuf[h, 0].reshape(PREFIX, 128)
            values = kvbuf[h, 1].reshape(PREFIX, 128)
            old = dot(q, keys, NT) + bias[0:1, :]
            new = jnp.where(causal, dot(q, newbuf[0, :, head_cols], NT), HIDDEN)
            top = jnp.maximum(
                jnp.max(old, axis=1, keepdims=True), jnp.max(new, axis=1, keepdims=True)
            )
            shift = top * EXP2_SCALE
            old = jnp.exp2(old * EXP2_SCALE - shift)
            new = jnp.exp2(new * EXP2_SCALE - shift)
            totals = jnp.sum(old, axis=1, keepdims=True) + jnp.sum(new, axis=1, keepdims=True)
            mixed = dot(old.astype(BF16), values) + dot(
                new.astype(BF16), newbuf[1, :, head_cols]
            )
            obuf[:, pl.ds(pl.multiple_of(qh * 128, 128), 128)] = (mixed / totals).astype(BF16)

        width = QHALF // PHASES
        src_cols = pl.ds(p * width, width)
        dst_cols = pl.ds(pl.multiple_of(myc * QHALF + p * width, width), width)
        pltpu.make_async_copy(
            obuf.at[my_rows, src_cols], attn_v.at[:, dst_cols], recv.at[R_OUT]
        ).start()
        remote(
            obuf.at[pl.ds(pl.multiple_of((1 - myc) * TOK, TOK), TOK), src_cols],
            attn_v.at[:, dst_cols],
            send.at[S_OUT],
            recv.at[R_OUT],
            {"dev": other},
        ).start()

    wait_for(dtbuf, recv.at[R_DT])
    wait_for(states.at[pl.ds(0, NG - 1)], recv.at[R_ST])
    for dx in range(NX):
        wait_for(bcbuf.at[lax.rem(myx + NX - dx, NX), 1 - myc], recv_c.at[dx])

    for r in range(REQ):
        for c in range(NC):
            dt_rows[2 * r : 2 * r + 2, c * TOK : (c + 1) * TOK] = dtbuf[r % NZ, r // NZ, c]
    odd_row = lax.broadcasted_iota(jnp.int32, (2 * REQ, NEW), 0) % 2 == 1
    rate = -jnp.exp(
        jnp.where(odd_row, jnp.full((2 * REQ, NEW), a_log[1]), jnp.full((2 * REQ, NEW), a_log[0]))
    )
    earlier = lax.broadcasted_iota(jnp.int32, (NEW, NEW), 0)
    later = lax.broadcasted_iota(jnp.int32, (NEW, NEW), 1)
    cumulative = dot(
        dt_rows[...] * (rate * LOG2E),
        (earlier <= later).astype(F32),
        precision=lax.Precision.HIGHEST,
    )
    less_step = cumulative - jnp.log2(dt_rows[...])
    for r in range(REQ):
        by_req[r, 0:2, :] = cumulative[2 * r : 2 * r + 2]
        by_req[r, 2:4, :] = less_step[2 * r : 2 * r + 2]

    second = lax.broadcasted_iota(jnp.int32, (1, 128), 1) >= 64
    skip = jnp.where(second, jnp.full((1, 128), d_skip[1]), jnp.full((1, 128), d_skip[0]))
    keep_second = second.astype(F32).astype(BF16)
    keep_first = (1.0 - second.astype(F32)).astype(BF16)
    low_half = lax.broadcasted_iota(jnp.int32, (128, 1), 0) < 64
    term = lax.broadcasted_iota(jnp.int32, (32, 4 * TOK), 0)
    lane = lax.broadcasted_iota(jnp.int32, (32, 4 * TOK), 1)
    wanted = jnp.where(lane < 2 * TOK, lane // TOK, 2 + lane // 64 - 4)
    chosen = ((term % 8 == wanted) & (term < 24)).astype(F32).astype(BF16)
    diagonal = lax.broadcasted_iota(jnp.int32, (TOK, TOK), 0) >= lax.broadcasted_iota(
        jnp.int32, (TOK, TOK), 1
    )

    def ssd_request(rx, rz):
        r = rx * NZ + rz
        x = jnp.concatenate([xbuf[rz, rx, 0], xbuf[rz, rx, 1]], axis=0)
        bc = jnp.concatenate([bcbuf[rx, 0, rz], bcbuf[rx, 1, rz]], axis=0)
        b, c = bc[:, :128], bc[:, 128:]
        kept = states[lax.div(owners[r], 16), lax.rem(owners[r], 16)]
        cum = by_req[r, 0:2, :]
        shifted = by_req[r, 2:4, :]
        last = cum[:, NEW - 1 :]
        rows = jnp.concatenate([cum, jnp.exp2(cum), jnp.exp2(last - shifted), cum], axis=0)
        high = rows.astype(BF16)
        left_over = rows - high.astype(F32)
        middle = left_over.astype(BF16)
        low = (left_over - middle.astype(F32)).astype(BF16)
        wide = dot(jnp.concatenate([high, middle, low, low], axis=0), chosen, TN)
        growth, gain = wide[:, 2 * TOK : 3 * TOK], wide[:, 3 * TOK :]
        inner_first = dot(c[:TOK], b[:TOK], NT)
        inner_second = dot(c[TOK:], b, NT)

        def decayed(h, inner, i, j):
            diff = (
                wide[i * TOK : (i + 1) * TOK, h * TOK : (h + 1) * TOK]
                - shifted[h : h + 1, j * TOK : (j + 1) * TOK]
            )
            if i == j:
                diff = jnp.where(diagonal, diff, HIDDEN)
            return (jnp.exp2(diff) * inner).astype(BF16)

        upper, lower = [], []
        for h in range(2):
            upper.append(decayed(h, inner_first, 0, 0))
            lower.append(decayed(h, inner_second[:, :TOK], 1, 0))
            lower.append(decayed(h, inner_second[:, TOK:], 1, 1))
        x_first = x * keep_first
        x_second = x * keep_second
        within = jnp.concatenate(
            [
                dot(
                    jnp.concatenate(upper, axis=1),
                    jnp.concatenate([x_first[:TOK], x_second[:TOK]], axis=0),
                ),
                dot(
                    jnp.concatenate(lower, axis=1), jnp.concatenate([x_first, x_second], axis=0)
                ),
            ],
            axis=0,
        )
        x_float = x.astype(F32)
        carried = growth * dot(c, kept, NT)
        ssd_v[pl.ds(pl.multiple_of(r * NEW, NEW), NEW), :] = (
            within + carried + skip * x_float
        ).astype(BF16)
        weighted = (x_float * gain).astype(BF16)
        total = jnp.exp2(last)
        left = jnp.where(
            low_half,
            jnp.broadcast_to(total[0:1], (128, 1)),
            jnp.broadcast_to(total[1:2], (128, 1)),
        )
        fin_v[r] = dot(weighted, b, TN) + left * kept.astype(F32)

    @pl.loop(0, NZ)
    def _(i):
        j = lax.rem(i + NZ - 1, NZ)
        odd = lax.rem(j, 2)
        dz = 4 + (1 - odd) * lax.div(j, 2) - odd * lax.div(j + 1, 2)
        rz = lax.rem(myz + NZ - dz, NZ)
        wait_for(xbuf.at[rz], recv_x.at[dz])

        for rx in range(NX):
            ssd_request(rx, rz)

    wait_for(attn_v, recv.at[R_OUT])
    wait_for(xbuf.at[pl.ds(0, NZ - 1)], send.at[S_X])
    wait_for(xbuf.at[0, pl.ds(0, NX - 1)], send.at[S_X])
    wait_for(xbuf.at[0, 0, 0], send.at[S_X])
    wait_for(dtbuf.at[pl.ds(0, NZ - 1)], send.at[S_DT])
    wait_for(dtbuf.at[0, pl.ds(0, NX - 1)], send.at[S_DT])
    wait_for(dtbuf.at[0, 0, 0], send.at[S_DT])
    wait_for(states.at[pl.ds(0, NG - 1)], send.at[S_ST])
    wait_for(qbuf.at[pl.ds(0, TOK)], send.at[S_Q])
    wait_for(newbuf.at[0], send.at[S_NK])
    wait_for(bcbuf.at[0, 0, pl.ds(0, NZ - 1)], send.at[S_BC])
    for pages in held[0] + held[1]:
        wait_for(pages, send.at[S_PG])
    wait_for(bcbuf.at[pl.ds(0, NX - 1), 0], send.at[S_BX])
    wait_for(bcbuf.at[:, 0], send.at[S_CORE])
    wait_for(obuf.at[pl.ds(0, TOK)], send.at[S_OUT])
    wait_for(stage.at[pl.ds(0, 7)], send.at[S_KV])
    wait_for(stage.at[0, 0], send.at[S_KV])
    wait_for(stage.at[0, 0, 0], send.at[S_KV])


def hand_over(*refs):
    sources, targets, sem = refs[:3], refs[3:6], refs[6]
    for i in range(3):
        rows = sources[i].shape[0] // PIECES
        for part in range(PIECES):
            piece = pl.ds(part * rows, rows)
            pltpu.make_async_copy(sources[i].at[piece], targets[i].at[piece], sem.at[i]).start()
    for i in range(3):
        pltpu.make_async_copy(sources[i], targets[i], sem.at[i]).wait()


def on_device(
    x_rows,
    dt_rows,
    bc_rows,
    a_log,
    d_skip,
    state_pool,
    owners,
    queries,
    new_kv,
    page_pool,
    page_table,
    prefix_len,
):
    smem = pl.BlockSpec(memory_space=pltpu.SMEM)
    vmem = pl.BlockSpec(memory_space=pltpu.VMEM)
    hbm = pl.BlockSpec(memory_space=pl.ANY)
    dma = pltpu.SemaphoreType.DMA
    ssd_out, finals, attn_out = pl.pallas_call(
        kernel,
        out_shape=(
            pltpu.VMEM((REQ * NEW, 128), BF16),
            pltpu.VMEM((REQ, 128, 128), F32),
            pltpu.VMEM((TOK, 2 * QHALF), BF16),
        ),
        in_specs=[smem] * 4 + [vmem, vmem, hbm, hbm, vmem, hbm, hbm, hbm],
        out_specs=(vmem, vmem, vmem),
        scratch_shapes=[
            pltpu.VMEM((NZ, NX, NC, TOK, 128), BF16),
            pltpu.VMEM((NZ, NX, NC, 2, TOK), F32),
            pltpu.VMEM((NX, NC, NZ, TOK, 256), BF16),
            pltpu.VMEM((NG, 16, 128, 128), BF16),
            *[pltpu.VMEM((HELD, PAGE, 4 * HALF), BF16)] * 5,
            pltpu.VMEM((ROUTES, NX, NC, HEADS_CORE, 2, PAGE, 128), BF16),
            pltpu.VMEM((HEADS_CORE, 2, NX, NC, NZ, PAGE, 128), BF16),
            pltpu.VMEM((NEW, QHALF), BF16),
            pltpu.VMEM((2, NEW, HALF), BF16),
            pltpu.VMEM((NEW, QHALF), BF16),
            pltpu.VMEM((REQ, 8, NEW), F32),
            pltpu.VMEM((2 * REQ, NEW), F32),
            pltpu.VMEM((NDEV, 2, TOK), F32),
            pltpu.VMEM((REQ, 128), jnp.int32),
            pltpu.SMEM((REQ, 128), jnp.int32),
            pltpu.VMEM((8, PREFIX), F32),
            dma((8,)),
            dma((11,)),
            dma((2, 4)),
            dma((2, 2, PARTS)),
            dma((NZ,)),
            dma((NX,)),
            dma((NX,)),
            dma((1,)),
        ],
        compiler_params=pltpu.CompilerParams(
            collective_id=0, has_side_effects=True, vmem_limit_bytes=54 * 1024 * 1024
        ),
    )(
        owners,
        a_log,
        d_skip,
        prefix_len,
        page_table,
        dt_rows,
        x_rows,
        bc_rows,
        state_pool.reshape(16, 128, 128),
        queries,
        new_kv,
        page_pool,
    )
    outs = (ssd_out, finals, attn_out)
    ssd_out, finals, attn_out = pl.pallas_call(
        hand_over,
        out_shape=tuple(jax.ShapeDtypeStruct(a.shape, a.dtype) for a in outs),
        in_specs=[vmem] * 3,
        out_specs=(hbm,) * 3,
        scratch_shapes=[dma((3,))],
        compiler_params=pltpu.CompilerParams(vmem_limit_bytes=40 * 1024 * 1024),
    )(*outs)
    return ssd_out, finals.reshape(REQ, 2, 64, 128), attn_out


def solution(mesh):
    return jax.shard_map(
        on_device,
        mesh=mesh,
        in_specs=(
            P(("grp", "dev"), None),
            P(("grp", "dev"), None),
            P(("grp", "dev"), None),
            P("dev"),
            P("dev"),
            P("grp", "dev", None, None),
            P("grp"),
            P(("grp", "dev"), None),
            P(("grp", "dev"), None),
            P(("grp", "dev"), None, None),
            P("grp", None),
            P("grp"),
        ),
        out_specs=(P("grp", "dev"), P("grp", "dev", None, None), P(("grp", "dev"), None)),
        check_vma=False,
    )
```

```python
import math

import jax
import jax.numpy as jnp
from jax import lax
from jax.experimental import pallas as pl
from jax.experimental.pallas import tpu as pltpu
from jax.sharding import PartitionSpec as P

MESH = pl.DeviceIdType.MESH
F32, BF16 = jnp.float32, jnp.bfloat16
NX, NZ, NC, NG = 4, 8, 2, 4
NDEV = NX * NZ * NC
REQ = 32
TOK = 128
NEW = 2 * TOK
HEADS_CORE = 4
QPER = 4
PAGE = 16
HELD = 8
PARTS = 1
ROUTES = 9
PREFIX = 1024
HALF = HEADS_CORE * 128
QHALF = HEADS_CORE * QPER * 128
PHASES = 2
PER_PHASE = HEADS_CORE // PHASES
LOG2E = math.log2(math.e)
EXP2_SCALE = LOG2E / math.sqrt(128.0)
HIDDEN = -1e30

NT = (((1,), (1,)), ((), ()))
TN = (((0,), (0,)), ((), ()))


def dot(a, b, dims=(((1,), (0,)), ((), ())), precision=None):
    return lax.dot_general(a, b, dims, precision=precision, preferred_element_type=F32)


def ssd_constants(d_skip):
    second = lax.broadcasted_iota(jnp.int32, (1, 128), 1) >= 64
    skip = jnp.where(second, jnp.full((1, 128), d_skip[1]), jnp.full((1, 128), d_skip[0]))
    keep_second = second.astype(F32).astype(BF16)
    keep_first = (1.0 - second.astype(F32)).astype(BF16)
    low_half = lax.broadcasted_iota(jnp.int32, (128, 1), 0) < 64
    term = lax.broadcasted_iota(jnp.int32, (32, 4 * TOK), 0)
    lane = lax.broadcasted_iota(jnp.int32, (32, 4 * TOK), 1)
    wanted = jnp.where(lane < 2 * TOK, lane // TOK, 2 + lane // 64 - 4)
    chosen = ((term % 8 == wanted) & (term < 24)).astype(F32).astype(BF16)
    diagonal = lax.broadcasted_iota(jnp.int32, (TOK, TOK), 0) >= lax.broadcasted_iota(
        jnp.int32, (TOK, TOK), 1
    )
    return second, skip, keep_first, keep_second, low_half, diagonal, chosen


def ssd_request(consts, by_req, xbuf, bcbuf, states, owners, rx, rz):
    second, skip, keep_first, keep_second, low_half, diagonal, chosen = consts
    r = rx * NZ + rz
    x = jnp.concatenate([xbuf[rz, rx, 0], xbuf[rz, rx, 1]], axis=0)
    bc = jnp.concatenate([bcbuf[rx, 0, rz], bcbuf[rx, 1, rz]], axis=0)
    b, c = bc[:, :128], bc[:, 128:]
    kept = states[lax.div(owners[r], 16), lax.rem(owners[r], 16)]
    cum = by_req[r, 0:2, :]
    shifted = by_req[r, 2:4, :]
    last = cum[:, NEW - 1 :]
    rows = jnp.concatenate([cum, jnp.exp2(cum), jnp.exp2(last - shifted), cum], axis=0)
    high = rows.astype(BF16)
    left_over = rows - high.astype(F32)
    middle = left_over.astype(BF16)
    low = (left_over - middle.astype(F32)).astype(BF16)
    wide = dot(jnp.concatenate([high, middle, low, low], axis=0), chosen, TN)
    growth, gain = wide[:, 2 * TOK : 3 * TOK], wide[:, 3 * TOK :]
    inner_first = dot(c[:TOK], b[:TOK], NT)
    inner_second = dot(c[TOK:], b, NT)

    def decayed(h, inner, i, j):
        diff = (
            wide[i * TOK : (i + 1) * TOK, h * TOK : (h + 1) * TOK]
            - shifted[h : h + 1, j * TOK : (j + 1) * TOK]
        )
        if i == j:
            diff = jnp.where(diagonal, diff, HIDDEN)
        return (jnp.exp2(diff) * inner).astype(BF16)

    upper, lower = [], []
    for h in range(2):
        upper.append(decayed(h, inner_first, 0, 0))
        lower.append(decayed(h, inner_second[:, :TOK], 1, 0))
        lower.append(decayed(h, inner_second[:, TOK:], 1, 1))
    x_first = x * keep_first
    x_second = x * keep_second
    within = jnp.concatenate(
        [
            dot(
                jnp.concatenate(upper, axis=1),
                jnp.concatenate([x_first[:TOK], x_second[:TOK]], axis=0),
            ),
            dot(
                jnp.concatenate(lower, axis=1), jnp.concatenate([x_first, x_second], axis=0)
            ),
        ],
        axis=0,
    )
    x_float = x.astype(F32)
    carried = growth * dot(c, kept, NT)
    mixed = (within + carried + skip * x_float).astype(BF16)
    weighted = (x_float * gain).astype(BF16)
    total = jnp.exp2(last)
    left = jnp.where(
        low_half,
        jnp.broadcast_to(total[0:1], (128, 1)),
        jnp.broadcast_to(total[1:2], (128, 1)),
    )
    return mixed, dot(weighted, b, TN) + left * kept.astype(F32)


def kernel(
    owners,
    a_log,
    d_skip,
    prefix_len,
    table_in,
    dt_in,
    x_in,
    bc_in,
    pool_in,
    q_in,
    kv_in,
    pages_in,
    ssd_v,
    fin_v,
    attn_v,
    xbuf,
    bcbuf,
    states,
    by_req,
    dtbuf,
    pool_own,
    up_near,
    up_far,
    down_near,
    down_far,
    stage,
    kvbuf,
    qbuf,
    newbuf,
    obuf,
    dt_rows,
    dt_stage,
    slots_v,
    slots,
    bias,
    recv,
    send,
    ring_bc,
    ring_pg,
    recv_x,
    recv_bx,
    recv_c,
    out_sem,
):
    grp = lax.axis_index("grp")
    me = lax.axis_index("dev")
    myx, myz, myc = lax.div(me, NZ * NC), lax.rem(lax.div(me, NC), NZ), lax.rem(me, NC)
    other = me + 1 - 2 * myc

    def peer(step):
        x = lax.rem(myx + lax.div(step, NZ * NC), NX)
        z = lax.rem(myz + lax.div(step, NC), NZ)
        return (x * NZ + z) * NC + lax.rem(myc + step, NC)

    def remote(src, dst, send_sem, recv_sem, where):
        return pltpu.make_async_remote_copy(
            src_ref=src,
            dst_ref=dst,
            send_sem=send_sem,
            recv_sem=recv_sem,
            device_id=where,
            device_id_type=MESH,
        )

    def wait_for(ref, sem):
        pltpu.make_async_copy(ref, ref, sem).wait()

    R_DT, R_ST, R_Q, R_NK, R_BC, R_PG, R_KV, R_OUT = range(8)
    S_X, S_DT, S_ST, S_Q, S_NK, S_BC, S_PG, S_BX, S_KV, S_CORE, S_OUT = range(11)

    barrier = pltpu.get_barrier_semaphore()

    @pl.loop(1, NDEV, unroll=9)
    def _(step):
        pl.semaphore_signal(
            barrier,
            inc=1,
            device_id={"dev": lax.rem(me + step, NDEV)},
            device_id_type=MESH,
        )

    for dg in range(1, NG):
        pl.semaphore_signal(
            barrier, inc=1, device_id={"grp": (grp + dg) % NG}, device_id_type=MESH
        )

    pl.semaphore_wait(barrier, NDEV - 1 + NG - 1)

    def on_ring(dz):
        return lax.rem(myz + dz + NZ, NZ)

    def at(x, z, c):
        return {"dev": (x * NZ + z) * NC + c}

    def map_rows(side):
        return pl.ds(side * (TOK // 2), TOK // 2)

    def page_rows(part):
        return pl.ds(part * (HELD // PARTS), HELD // PARTS)

    ways = (1, -1)
    held = ((up_near, up_far), (down_near, down_far))

    def pass_maps(step, side, source, distance=1, rows=None):
        block = bcbuf.at[myx, myc, on_ring(-min(step - 1, 2) * ways[side])]
        if rows is not None:
            block = block.at[rows]
        remote(
            block if source is None else source,
            block,
            send.at[S_BC],
            ring_bc.at[side, step - 1],
            at(myx, on_ring(distance * ways[side]), myc),
        ).start()

    def pass_pages(step, side, part):
        source = pages_in if step == 1 else held[side][0]
        remote(
            source.at[page_rows(part)],
            held[side][step - 1].at[page_rows(part)],
            send.at[S_PG],
            ring_pg.at[side, step - 1, part],
            at(myx, on_ring(ways[side]), myc),
        ).start()

    for side in range(2):
        pass_maps(1, side, bc_in)
    for part in range(PARTS):
        for side in range(2):
            pass_pages(1, side, part)
    own_pages = pltpu.make_async_copy(pages_in, pool_own, recv.at[R_PG])
    own_pages.start()
    own_maps = pltpu.make_async_copy(bc_in, bcbuf.at[myx, myc, myz], recv.at[R_BC])
    own_maps.start()

    def send_x(dz, k):
        x = lax.rem(myx + lax.div(k, NC), NX)
        to = (x * NZ + lax.rem(myz + dz, NZ)) * NC + lax.rem(myc + k, NC)
        remote(
            x_in.at[:, pl.ds(pl.multiple_of(to * 128, 128), 128)],
            xbuf.at[myz, myx, myc],
            send.at[S_X],
            recv_x.at[dz],
            {"dev": to},
        ).start()

    pltpu.make_async_copy(
        x_in.at[:, pl.ds(pl.multiple_of(me * 128, 128), 128)],
        xbuf.at[myz, myx, myc],
        recv_x.at[0],
    ).start()

    @pl.loop(1, NX * NC)
    def _(k):
        send_x(0, k)

    holder, place = lax.shift_right_logical(table_in[...], 3), table_in[...] & (HELD - 1)
    lane = lax.broadcasted_iota(jnp.int32, (REQ, 128), 1)
    found = jnp.zeros((REQ, 128), jnp.int32)
    for z in range(NZ):
        line = (myx * NZ + z) * NC + myc
        here = jnp.sum(jnp.where(holder == line, place, 0), axis=1, keepdims=True)
        found = jnp.where(lane == z, here, found)
    slots_v[...] = found
    to_smem = pltpu.make_async_copy(slots_v, slots, out_sem.at[0])
    to_smem.start()

    by_head = dt_in[...].astype(F32).T
    for pair in range(NDEV):
        dt_stage[pair] = by_head[2 * pair : 2 * pair + 2]
    states[grp] = pool_in[...].astype(BF16)

    for dg in range(1, NG):
        remote(
            states.at[grp],
            states.at[grp],
            send.at[S_ST],
            recv.at[R_ST],
            {"grp": lax.rem(grp + dg, NG)},
        ).start()

    pltpu.make_async_copy(dt_stage.at[me], dtbuf.at[myz, myx, myc], recv.at[R_DT]).start()

    @pl.loop(1, NDEV)
    def _(step):
        to = peer(step)
        remote(
            dt_stage.at[to], dtbuf.at[myz, myx, myc], send.at[S_DT], recv.at[R_DT], {"dev": to}
        ).start()

    def send_both_ways(near):
        @pl.loop(0, 2 * NX * NC)
        def _(i):
            send_x(near + lax.rem(i, 2) * (NZ - 2 * near), lax.div(i, 2))

    def send_far():
        @pl.loop(0, NX * NC)
        def _(k):
            send_x(4, k)

    my_rows = pl.ds(pl.multiple_of(myc * TOK, TOK), TOK)

    def half(ref, start, width, core):
        return ref.at[:, pl.ds(pl.multiple_of(start + core * width, width), width)]

    pltpu.make_async_copy(half(q_in, 0, QHALF, myc), qbuf.at[my_rows], recv.at[R_Q]).start()
    remote(
        half(q_in, 0, QHALF, 1 - myc),
        qbuf.at[my_rows],
        send.at[S_Q],
        recv.at[R_Q],
        {"dev": other},
    ).start()
    for kv in range(2):
        pltpu.make_async_copy(
            half(kv_in, kv * 2 * HALF, HALF, myc), newbuf.at[kv, my_rows], recv.at[R_NK]
        ).start()
        remote(
            half(kv_in, kv * 2 * HALF, HALF, 1 - myc),
            newbuf.at[kv, my_rows],
            send.at[S_NK],
            recv.at[R_NK],
            {"dev": other},
        ).start()

    def spread_maps(z):
        block = bcbuf.at[myx, myc, z]
        for dx in range(1, NX):
            remote(
                block,
                block,
                send.at[S_BX],
                recv_bx.at[dx],
                at(lax.rem(myx + dx, NX), myz, myc),
            ).start()

    def spread_pages(place, pages, away, onward=0, cores=(0, 1)):
        z, target = on_ring(away), on_ring(onward)
        mine = kvbuf.at[:, :, myx, myc, z]

        @pl.loop(0, NX)
        def _(x):
            slot = slots[x * NZ + target, z]
            for kv in range(2):
                for c in cores:
                    for hh in range(HEADS_CORE):
                        col = ((kv * 2 + c) * HEADS_CORE + hh) * 128
                        stage[place, x, c, hh, kv] = pages[slot, :, col : col + 128]

        def pages_to(x, c):
            remote(
                stage.at[place, x, c], mine, send.at[S_KV], recv.at[R_KV], at(x, target, c)
            ).start()

        if onward == 0:
            pltpu.make_async_copy(stage.at[place, myx, myc], mine, recv.at[R_KV]).start()

            @pl.loop(1, NX * NC)
            def _(k):
                pages_to(lax.rem(myx + lax.div(k, NC), NX), lax.rem(myc + k, NC))
        elif len(cores) == 2:

            @pl.loop(0, NX * NC)
            def _(k):
                pages_to(lax.rem(myx + lax.div(k, NC), NX), lax.rem(myc + k, NC))
        else:

            @pl.loop(0, NX)
            def _(dx):
                pages_to(lax.rem(myx + dx, NX), cores[0])

    mine = lax.broadcasted_iota(jnp.int32, (REQ, NDEV), 0) == lax.div(me, NC)
    my_holders = jnp.sum(jnp.where(mine, holder.astype(F32), 0.0), axis=0, keepdims=True)
    block = lax.broadcasted_iota(jnp.int32, (NDEV, NDEV), 0)
    block_holder = (
        (block // (NC * NZ)) * (NC * NZ) + (block % NZ) * NC + (block // NZ) % NC
    ).astype(F32)
    entry = lax.broadcasted_iota(jnp.int32, (8, NDEV), 1).astype(F32)
    found_at = dot(entry, (my_holders == block_holder).astype(F32), NT)
    key = lax.broadcasted_iota(jnp.int32, (NDEV, PREFIX), 1)
    spread = (key // PAGE == lax.broadcasted_iota(jnp.int32, (NDEV, PREFIX), 0)).astype(F32)
    position = dot(found_at, spread) * PAGE + (
        lax.broadcasted_iota(jnp.int32, (8, PREFIX), 1) % PAGE
    ).astype(F32)
    length = jnp.full((8, PREFIX), prefix_len[lax.div(me, NC)]).astype(F32)
    bias[...] = jnp.where(position < length, 0.0, HIDDEN)

    to_smem.wait()
    own_maps.wait()
    spread_maps(myz)
    own_pages.wait()
    spread_pages(0, pool_own, 0)
    for step in (1, 2):
        for side in range(2):
            z = on_ring(-step * ways[side])
            wait_for(bcbuf.at[myx, myc, z], ring_bc.at[side, step - 1])
            pass_maps(step + 1, side, None)
            if step == 2:
                pass_maps(4, side, None, 2, map_rows(side))
        for part in range(PARTS):
            for side in range(2):
                wait_for(
                    held[side][step - 1].at[page_rows(part)], ring_pg.at[side, step - 1, part]
                )
                if step == 1:
                    pass_pages(2, side, part)
        for side in range(2):
            spread_maps(on_ring(-step * ways[side]))
        if step == 2:
            for side in range(2):
                spread_pages(5 + side, held[side][1], -2 * ways[side], 2 * ways[side], (side,))
            for side in range(2):
                spread_pages(7 + side, held[side][1], -2 * ways[side], ways[side])
        for side in range(2):
            spread_pages(2 * step - 1 + side, held[side][step - 1], -step * ways[side])

    for side in range(2):
        z = on_ring(-3 * ways[side])
        wait_for(bcbuf.at[myx, myc, z], ring_bc.at[side, 2])
        spread_maps(z)
    far = on_ring(4)
    for side in range(2):
        wait_for(bcbuf.at[myx, myc, far, map_rows(side)], ring_bc.at[side, 3])
    spread_maps(far)
    send_far()
    send_both_ways(3)

    def maps_to_other_core():
        for dx in range(NX):
            block = bcbuf.at[lax.rem(myx + NX - dx, NX), myc]
            if dx:
                wait_for(block, recv_bx.at[dx])
            remote(block, block, send.at[S_CORE], recv_c.at[dx], {"dev": other}).start()

    maps_to_other_core()
    send_both_ways(2)
    send_both_ways(1)
    wait_for(qbuf, recv.at[R_Q])
    wait_for(newbuf, recv.at[R_NK])
    wait_for(kvbuf, recv.at[R_KV])
    causal = lax.broadcasted_iota(jnp.int32, (NEW, NEW), 0) >= lax.broadcasted_iota(
        jnp.int32, (NEW, NEW), 1
    )
    for p in range(PHASES):
        @pl.loop(p * PER_PHASE * QPER, (p + 1) * PER_PHASE * QPER)
        def _(qh):
            h = lax.div(qh, QPER)
            head_cols = pl.ds(pl.multiple_of(h * 128, 128), 128)
            q = qbuf[:, pl.ds(pl.multiple_of(qh * 128, 128), 128)]
            keys = kvbuf[h, 0].reshape(PREFIX, 128)
            values = kvbuf[h, 1].reshape(PREFIX, 128)
            old = dot(q, keys, NT) + bias[0:1, :]
            new = jnp.where(causal, dot(q, newbuf[0, :, head_cols], NT), HIDDEN)
            top = jnp.maximum(
                jnp.max(old, axis=1, keepdims=True), jnp.max(new, axis=1, keepdims=True)
            )
            shift = top * EXP2_SCALE
            old = jnp.exp2(old * EXP2_SCALE - shift)
            new = jnp.exp2(new * EXP2_SCALE - shift)
            totals = jnp.sum(old, axis=1, keepdims=True) + jnp.sum(new, axis=1, keepdims=True)
            mixed = dot(old.astype(BF16), values) + dot(
                new.astype(BF16), newbuf[1, :, head_cols]
            )
            obuf[:, pl.ds(pl.multiple_of(qh * 128, 128), 128)] = (mixed / totals).astype(BF16)

        width = QHALF // PHASES
        src_cols = pl.ds(p * width, width)
        dst_cols = pl.ds(pl.multiple_of(myc * QHALF + p * width, width), width)
        pltpu.make_async_copy(
            obuf.at[my_rows, src_cols], attn_v.at[:, dst_cols], recv.at[R_OUT]
        ).start()
        remote(
            obuf.at[pl.ds(pl.multiple_of((1 - myc) * TOK, TOK), TOK), src_cols],
            attn_v.at[:, dst_cols],
            send.at[S_OUT],
            recv.at[R_OUT],
            {"dev": other},
        ).start()

    wait_for(dtbuf, recv.at[R_DT])
    wait_for(states.at[pl.ds(0, NG - 1)], recv.at[R_ST])
    for dx in range(NX):
        wait_for(bcbuf.at[lax.rem(myx + NX - dx, NX), 1 - myc], recv_c.at[dx])

    for r in range(REQ):
        for c in range(NC):
            dt_rows[2 * r : 2 * r + 2, c * TOK : (c + 1) * TOK] = dtbuf[r % NZ, r // NZ, c]
    odd_row = lax.broadcasted_iota(jnp.int32, (2 * REQ, NEW), 0) % 2 == 1
    rate = -jnp.exp(
        jnp.where(odd_row, jnp.full((2 * REQ, NEW), a_log[1]), jnp.full((2 * REQ, NEW), a_log[0]))
    )
    earlier = lax.broadcasted_iota(jnp.int32, (NEW, NEW), 0)
    later = lax.broadcasted_iota(jnp.int32, (NEW, NEW), 1)
    cumulative = dot(
        dt_rows[...] * (rate * LOG2E),
        (earlier <= later).astype(F32),
        precision=lax.Precision.HIGHEST,
    )
    less_step = cumulative - jnp.log2(dt_rows[...])
    for r in range(REQ):
        by_req[r, 0:2, :] = cumulative[2 * r : 2 * r + 2]
        by_req[r, 2:4, :] = less_step[2 * r : 2 * r + 2]

    consts = ssd_constants(d_skip)

    @pl.loop(0, NZ - 2)
    def _(i):
        j = lax.rem(i + NZ - 3, NZ - 2)
        odd = lax.rem(j, 2)
        dz = 4 + (1 - odd) * lax.div(j, 2) - odd * lax.div(j + 1, 2)
        dz = dz * lax.div(i + NZ - 1, NZ)
        rz = lax.rem(myz + NZ - dz, NZ)
        wait_for(xbuf.at[rz], recv_x.at[dz])
        for rx in range(NX):
            r = rx * NZ + rz
            rows = pl.ds(pl.multiple_of(r * NEW, NEW), NEW)
            ssd_v[rows, :], fin_v[r] = ssd_request(
                consts, by_req, xbuf, bcbuf, states, owners, rx, rz
            )

    for dz in (1, NZ - 1):
        wait_for(xbuf.at[lax.rem(myz + NZ - dz, NZ)], recv_x.at[dz])

    wait_for(attn_v, recv.at[R_OUT])
    wait_for(xbuf.at[pl.ds(0, NZ - 1)], send.at[S_X])
    wait_for(xbuf.at[0, pl.ds(0, NX - 1)], send.at[S_X])
    wait_for(xbuf.at[0, 0, 0], send.at[S_X])
    wait_for(dtbuf.at[pl.ds(0, NZ - 1)], send.at[S_DT])
    wait_for(dtbuf.at[0, pl.ds(0, NX - 1)], send.at[S_DT])
    wait_for(dtbuf.at[0, 0, 0], send.at[S_DT])
    wait_for(states.at[pl.ds(0, NG - 1)], send.at[S_ST])
    wait_for(qbuf.at[pl.ds(0, TOK)], send.at[S_Q])
    wait_for(newbuf.at[0], send.at[S_NK])
    wait_for(bcbuf.at[0, 0, pl.ds(0, NZ - 1)], send.at[S_BC])
    for pages in held[0] + held[1]:
        wait_for(pages, send.at[S_PG])
    wait_for(bcbuf.at[pl.ds(0, NX - 1), 0], send.at[S_BX])
    wait_for(bcbuf.at[:, 0], send.at[S_CORE])
    wait_for(obuf.at[pl.ds(0, TOK)], send.at[S_OUT])
    wait_for(stage.at[pl.ds(0, 7)], send.at[S_KV])
    wait_for(stage.at[0, 0], send.at[S_KV])
    wait_for(stage.at[0, 0, 0], send.at[S_KV])


def hand_over(
    owners,
    d_skip,
    ssd_v,
    fin_v,
    attn_v,
    xbuf,
    bcbuf,
    states,
    by_req,
    ssd_out,
    fin_out,
    attn_out,
    ssd_last,
    fin_last,
    sem,
):
    myz = lax.rem(lax.div(lax.axis_index("dev"), NC), NZ)

    def rows_of(r):
        return pl.ds(pl.multiple_of(r * NEW, NEW), NEW)

    def write(ssd, fin, r):
        pltpu.make_async_copy(ssd, ssd_out.at[rows_of(r)], sem.at[0]).start()
        pltpu.make_async_copy(fin, fin_out.at[r], sem.at[1]).start()

    pltpu.make_async_copy(attn_v, attn_out, sem.at[2]).start()

    @pl.loop(0, NZ - 3)
    def _(i):
        for rx in range(NX):
            r = rx * NZ + lax.rem(myz + 2 + i, NZ)
            write(ssd_v.at[rows_of(r)], fin_v.at[r], r)

    for rx in range(NX):
        r = rx * NZ + myz
        write(ssd_v.at[rows_of(r)], fin_v.at[r], r)

    consts = ssd_constants(d_skip)

    @pl.loop(0, 2)
    def _(side):
        rz = lax.rem(myz + NZ - 1 + 2 * side, NZ)
        for rx in range(NX):
            ssd_last[side, rx], fin_last[side, rx] = ssd_request(
                consts, by_req, xbuf, bcbuf, states, owners, rx, rz
            )
        for rx in range(NX):
            write(ssd_last.at[side, rx], fin_last.at[side, rx], rx * NZ + rz)

    pltpu.make_async_copy(ssd_out, ssd_out, sem.at[0]).wait()
    pltpu.make_async_copy(fin_out, fin_out, sem.at[1]).wait()
    pltpu.make_async_copy(attn_v, attn_out, sem.at[2]).wait()


def on_device(
    x_rows,
    dt_rows,
    bc_rows,
    a_log,
    d_skip,
    state_pool,
    owners,
    queries,
    new_kv,
    page_pool,
    page_table,
    prefix_len,
):
    smem = pl.BlockSpec(memory_space=pltpu.SMEM)
    vmem = pl.BlockSpec(memory_space=pltpu.VMEM)
    hbm = pl.BlockSpec(memory_space=pl.ANY)
    dma = pltpu.SemaphoreType.DMA
    left = pl.pallas_call(
        kernel,
        out_shape=(
            pltpu.VMEM((REQ * NEW, 128), BF16),
            pltpu.VMEM((REQ, 128, 128), F32),
            pltpu.VMEM((TOK, 2 * QHALF), BF16),
            pltpu.VMEM((NZ, NX, NC, TOK, 128), BF16),
            pltpu.VMEM((NX, NC, NZ, TOK, 256), BF16),
            pltpu.VMEM((NG, 16, 128, 128), BF16),
            pltpu.VMEM((REQ, 8, NEW), F32),
        ),
        in_specs=[smem] * 4 + [vmem, vmem, hbm, hbm, vmem, hbm, hbm, hbm],
        out_specs=(vmem,) * 7,
        scratch_shapes=[
            pltpu.VMEM((NZ, NX, NC, 2, TOK), F32),
            *[pltpu.VMEM((HELD, PAGE, 4 * HALF), BF16)] * 5,
            pltpu.VMEM((ROUTES, NX, NC, HEADS_CORE, 2, PAGE, 128), BF16),
            pltpu.VMEM((HEADS_CORE, 2, NX, NC, NZ, PAGE, 128), BF16),
            pltpu.VMEM((NEW, QHALF), BF16),
            pltpu.VMEM((2, NEW, HALF), BF16),
            pltpu.VMEM((NEW, QHALF), BF16),
            pltpu.VMEM((2 * REQ, NEW), F32),
            pltpu.VMEM((NDEV, 2, TOK), F32),
            pltpu.VMEM((REQ, 128), jnp.int32),
            pltpu.SMEM((REQ, 128), jnp.int32),
            pltpu.VMEM((8, PREFIX), F32),
            dma((8,)),
            dma((11,)),
            dma((2, 4)),
            dma((2, 2, PARTS)),
            dma((NZ,)),
            dma((NX,)),
            dma((NX,)),
            dma((1,)),
        ],
        compiler_params=pltpu.CompilerParams(
            collective_id=0, has_side_effects=True, vmem_limit_bytes=46 * 1024 * 1024
        ),
    )(
        owners,
        a_log,
        d_skip,
        prefix_len,
        page_table,
        dt_rows,
        x_rows,
        bc_rows,
        state_pool.reshape(16, 128, 128),
        queries,
        new_kv,
        page_pool,
    )
    ssd_out, finals, attn_out = pl.pallas_call(
        hand_over,
        out_shape=tuple(jax.ShapeDtypeStruct(a.shape, a.dtype) for a in left[:3]),
        in_specs=[smem] * 2 + [vmem] * 7,
        out_specs=(hbm,) * 3,
        scratch_shapes=[
            pltpu.VMEM((2, NX, NEW, 128), BF16),
            pltpu.VMEM((2, NX, 128, 128), F32),
            dma((3,)),
        ],
        compiler_params=pltpu.CompilerParams(vmem_limit_bytes=16 * 1024 * 1024),
    )(owners, d_skip, *left)
    return ssd_out, finals.reshape(REQ, 2, 64, 128), attn_out


def solution(mesh):
    return jax.shard_map(
        on_device,
        mesh=mesh,
        in_specs=(
            P(("grp", "dev"), None),
            P(("grp", "dev"), None),
            P(("grp", "dev"), None),
            P("dev"),
            P("dev"),
            P("grp", "dev", None, None),
            P("grp"),
            P(("grp", "dev"), None),
            P(("grp", "dev"), None),
            P(("grp", "dev"), None, None),
            P("grp", None),
            P("grp"),
        ),
        out_specs=(P("grp", "dev"), P("grp", "dev", None, None), P(("grp", "dev"), None)),
        check_vma=False,
    )
```

```python
import math

import jax
import jax.numpy as jnp
from jax import lax
from jax.experimental import pallas as pl
from jax.experimental.pallas import tpu as pltpu
from jax.sharding import PartitionSpec as P

MESH = pl.DeviceIdType.MESH
F32, BF16 = jnp.float32, jnp.bfloat16
NX, NZ, NC, NG = 4, 8, 2, 4
NDEV = NX * NZ * NC
REQ = 32
TOK = 128
NEW = 2 * TOK
HEADS_CORE = 4
QPER = 4
PAGE = 16
HELD = 8
PARTS = 1
ROUTES = 9
PREFIX = 1024
HALF = HEADS_CORE * 128
QHALF = HEADS_CORE * QPER * 128
PHASES = 2
PER_PHASE = HEADS_CORE // PHASES
LOG2E = math.log2(math.e)
EXP2_SCALE = LOG2E / math.sqrt(128.0)
HIDDEN = -1e30

NT = (((1,), (1,)), ((), ()))
TN = (((0,), (0,)), ((), ()))


def dot(a, b, dims=(((1,), (0,)), ((), ())), precision=None):
    return lax.dot_general(a, b, dims, precision=precision, preferred_element_type=F32)


def ssd_constants(d_skip):
    second = lax.broadcasted_iota(jnp.int32, (1, 128), 1) >= 64
    skip = jnp.where(second, jnp.full((1, 128), d_skip[1]), jnp.full((1, 128), d_skip[0]))
    keep_second = second.astype(F32).astype(BF16)
    keep_first = (1.0 - second.astype(F32)).astype(BF16)
    low_half = lax.broadcasted_iota(jnp.int32, (128, 1), 0) < 64
    term = lax.broadcasted_iota(jnp.int32, (32, 4 * TOK), 0)
    lane = lax.broadcasted_iota(jnp.int32, (32, 4 * TOK), 1)
    wanted = jnp.where(lane < 2 * TOK, lane // TOK, 2 + lane // 64 - 4)
    chosen = ((term % 8 == wanted) & (term < 24)).astype(F32).astype(BF16)
    diagonal = lax.broadcasted_iota(jnp.int32, (TOK, TOK), 0) >= lax.broadcasted_iota(
        jnp.int32, (TOK, TOK), 1
    )
    return second, skip, keep_first, keep_second, low_half, diagonal, chosen


def ssd_request(consts, by_req, xbuf, bcbuf, states, owners, rx, rz):
    second, skip, keep_first, keep_second, low_half, diagonal, chosen = consts
    r = rx * NZ + rz
    x = jnp.concatenate([xbuf[rz, rx, 0], xbuf[rz, rx, 1]], axis=0)
    bc = jnp.concatenate([bcbuf[rx, 0, rz], bcbuf[rx, 1, rz]], axis=0)
    b, c = bc[:, :128], bc[:, 128:]
    kept = states[lax.div(owners[r], 16), lax.rem(owners[r], 16)]
    cum = by_req[r, 0:2, :]
    shifted = by_req[r, 2:4, :]
    last = cum[:, NEW - 1 :]
    rows = jnp.concatenate([cum, jnp.exp2(cum), jnp.exp2(last - shifted), cum], axis=0)
    high = rows.astype(BF16)
    left_over = rows - high.astype(F32)
    middle = left_over.astype(BF16)
    low = (left_over - middle.astype(F32)).astype(BF16)
    wide = dot(jnp.concatenate([high, middle, low, low], axis=0), chosen, TN)
    growth, gain = wide[:, 2 * TOK : 3 * TOK], wide[:, 3 * TOK :]
    inner_first = dot(c[:TOK], b[:TOK], NT)
    inner_second = dot(c[TOK:], b, NT)

    def decayed(h, inner, i, j):
        diff = (
            wide[i * TOK : (i + 1) * TOK, h * TOK : (h + 1) * TOK]
            - shifted[h : h + 1, j * TOK : (j + 1) * TOK]
        )
        if i == j:
            diff = jnp.where(diagonal, diff, HIDDEN)
        return (jnp.exp2(diff) * inner).astype(BF16)

    upper, lower = [], []
    for h in range(2):
        upper.append(decayed(h, inner_first, 0, 0))
        lower.append(decayed(h, inner_second[:, :TOK], 1, 0))
        lower.append(decayed(h, inner_second[:, TOK:], 1, 1))
    x_first = x * keep_first
    x_second = x * keep_second
    within = jnp.concatenate(
        [
            dot(
                jnp.concatenate(upper, axis=1),
                jnp.concatenate([x_first[:TOK], x_second[:TOK]], axis=0),
            ),
            dot(
                jnp.concatenate(lower, axis=1), jnp.concatenate([x_first, x_second], axis=0)
            ),
        ],
        axis=0,
    )
    x_float = x.astype(F32)
    carried = growth * dot(c, kept, NT)
    mixed = (within + carried + skip * x_float).astype(BF16)
    weighted = (x_float * gain).astype(BF16)
    total = jnp.exp2(last)
    left = jnp.where(
        low_half,
        jnp.broadcast_to(total[0:1], (128, 1)),
        jnp.broadcast_to(total[1:2], (128, 1)),
    )
    return mixed, dot(weighted, b, TN) + left * kept.astype(F32)


def kernel(
    owners,
    a_log,
    d_skip,
    prefix_len,
    table_in,
    dt_in,
    x_in,
    bc_in,
    pool_in,
    q_in,
    kv_in,
    pages_in,
    ssd_v,
    fin_v,
    attn_v,
    xbuf,
    bcbuf,
    states,
    by_req,
    dtbuf,
    pool_own,
    up_near,
    up_far,
    down_near,
    down_far,
    stage,
    kvbuf,
    qbuf,
    newbuf,
    obuf,
    dt_rows,
    dt_stage,
    slots_v,
    slots,
    bias,
    recv,
    send,
    ring_bc,
    ring_pg,
    recv_x,
    recv_bx,
    recv_c,
    out_sem,
):
    grp = lax.axis_index("grp")
    me = lax.axis_index("dev")
    myx, myz, myc = lax.div(me, NZ * NC), lax.rem(lax.div(me, NC), NZ), lax.rem(me, NC)
    other = me + 1 - 2 * myc

    def peer(step):
        x = lax.rem(myx + lax.div(step, NZ * NC), NX)
        z = lax.rem(myz + lax.div(step, NC), NZ)
        return (x * NZ + z) * NC + lax.rem(myc + step, NC)

    def remote(src, dst, send_sem, recv_sem, where):
        return pltpu.make_async_remote_copy(
            src_ref=src,
            dst_ref=dst,
            send_sem=send_sem,
            recv_sem=recv_sem,
            device_id=where,
            device_id_type=MESH,
        )

    def wait_for(ref, sem):
        pltpu.make_async_copy(ref, ref, sem).wait()

    R_DT, R_ST, R_Q, R_NK, R_BC, R_PG, R_KV, R_OUT = range(8)
    S_X, S_DT, S_ST, S_Q, S_NK, S_BC, S_PG, S_BX, S_KV, S_CORE, S_OUT = range(11)

    barrier = pltpu.get_barrier_semaphore()

    @pl.loop(1, NDEV, unroll=9)
    def _(step):
        pl.semaphore_signal(
            barrier,
            inc=1,
            device_id={"dev": lax.rem(me + step, NDEV)},
            device_id_type=MESH,
        )

    for dg in range(1, NG):
        pl.semaphore_signal(
            barrier, inc=1, device_id={"grp": (grp + dg) % NG}, device_id_type=MESH
        )

    pl.semaphore_wait(barrier, NDEV - 1 + NG - 1)

    def on_ring(dz):
        return lax.rem(myz + dz + NZ, NZ)

    def at(x, z, c):
        return {"dev": (x * NZ + z) * NC + c}

    def map_rows(side):
        return pl.ds(side * (TOK // 2), TOK // 2)

    def page_rows(part):
        return pl.ds(part * (HELD // PARTS), HELD // PARTS)

    ways = (1, -1)
    held = ((up_near, up_far), (down_near, down_far))

    def pass_maps(step, side, source, distance=1, rows=None):
        block = bcbuf.at[myx, myc, on_ring(-min(step - 1, 2) * ways[side])]
        if rows is not None:
            block = block.at[rows]
        remote(
            block if source is None else source,
            block,
            send.at[S_BC],
            ring_bc.at[side, step - 1],
            at(myx, on_ring(distance * ways[side]), myc),
        ).start()

    def pass_pages(step, side, part):
        source = pages_in if step == 1 else held[side][0]
        remote(
            source.at[page_rows(part)],
            held[side][step - 1].at[page_rows(part)],
            send.at[S_PG],
            ring_pg.at[side, step - 1, part],
            at(myx, on_ring(ways[side]), myc),
        ).start()

    for side in range(2):
        pass_maps(1, side, bc_in)
    for part in range(PARTS):
        for side in range(2):
            pass_pages(1, side, part)
    own_pages = pltpu.make_async_copy(pages_in, pool_own, recv.at[R_PG])
    own_pages.start()
    own_maps = pltpu.make_async_copy(bc_in, bcbuf.at[myx, myc, myz], recv.at[R_BC])
    own_maps.start()

    def send_x(dz, k):
        x = lax.rem(myx + lax.div(k, NC), NX)
        to = (x * NZ + lax.rem(myz + dz, NZ)) * NC + lax.rem(myc + k, NC)
        remote(
            x_in.at[:, pl.ds(pl.multiple_of(to * 128, 128), 128)],
            xbuf.at[myz, myx, myc],
            send.at[S_X],
            recv_x.at[dz],
            {"dev": to},
        ).start()

    pltpu.make_async_copy(
        x_in.at[:, pl.ds(pl.multiple_of(me * 128, 128), 128)],
        xbuf.at[myz, myx, myc],
        recv_x.at[0],
    ).start()

    @pl.loop(1, NX * NC)
    def _(k):
        send_x(0, k)

    holder, place = lax.shift_right_logical(table_in[...], 3), table_in[...] & (HELD - 1)
    lane = lax.broadcasted_iota(jnp.int32, (REQ, 128), 1)
    found = jnp.zeros((REQ, 128), jnp.int32)
    for z in range(NZ):
        line = (myx * NZ + z) * NC + myc
        here = jnp.sum(jnp.where(holder == line, place, 0), axis=1, keepdims=True)
        found = jnp.where(lane == z, here, found)
    slots_v[...] = found
    to_smem = pltpu.make_async_copy(slots_v, slots, out_sem.at[0])
    to_smem.start()

    by_head = dt_in[...].astype(F32).T
    for pair in range(NDEV):
        dt_stage[pair] = by_head[2 * pair : 2 * pair + 2]
    states[grp] = pool_in[...].astype(BF16)

    for dg in range(1, NG):
        remote(
            states.at[grp],
            states.at[grp],
            send.at[S_ST],
            recv.at[R_ST],
            {"grp": lax.rem(grp + dg, NG)},
        ).start()

    pltpu.make_async_copy(dt_stage.at[me], dtbuf.at[myz, myx, myc], recv.at[R_DT]).start()


    def send_both_ways(near):
        @pl.loop(0, 2 * NX * NC)
        def _(i):
            send_x(near + lax.rem(i, 2) * (NZ - 2 * near), lax.div(i, 2))

    def send_far():
        @pl.loop(0, NX * NC)
        def _(k):
            send_x(4, k)

    my_rows = pl.ds(pl.multiple_of(myc * TOK, TOK), TOK)

    def half(ref, start, width, core):
        return ref.at[:, pl.ds(pl.multiple_of(start + core * width, width), width)]

    pltpu.make_async_copy(half(q_in, 0, QHALF, myc), qbuf.at[my_rows], recv.at[R_Q]).start()
    remote(
        half(q_in, 0, QHALF, 1 - myc),
        qbuf.at[my_rows],
        send.at[S_Q],
        recv.at[R_Q],
        {"dev": other},
    ).start()
    for kv in range(2):
        pltpu.make_async_copy(
            half(kv_in, kv * 2 * HALF, HALF, myc), newbuf.at[kv, my_rows], recv.at[R_NK]
        ).start()
        remote(
            half(kv_in, kv * 2 * HALF, HALF, 1 - myc),
            newbuf.at[kv, my_rows],
            send.at[S_NK],
            recv.at[R_NK],
            {"dev": other},
        ).start()

    def spread_maps(z):
        block = bcbuf.at[myx, myc, z]
        for dx in range(1, NX):
            remote(
                block,
                block,
                send.at[S_BX],
                recv_bx.at[dx],
                at(lax.rem(myx + dx, NX), myz, myc),
            ).start()

    def spread_pages(place, pages, away, onward=0, cores=(0, 1)):
        z, target = on_ring(away), on_ring(onward)
        mine = kvbuf.at[:, :, myx, myc, z]

        @pl.loop(0, NX, unroll=True)
        def _(x):
            slot = slots[x * NZ + target, z]
            for kv in range(2):
                for c in cores:
                    for hh in range(HEADS_CORE):
                        col = ((kv * 2 + c) * HEADS_CORE + hh) * 128
                        stage[place, x, c, hh, kv] = pages[slot, :, col : col + 128]

        def pages_to(x, c):
            remote(
                stage.at[place, x, c], mine, send.at[S_KV], recv.at[R_KV], at(x, target, c)
            ).start()

        if onward == 0:
            pltpu.make_async_copy(stage.at[place, myx, myc], mine, recv.at[R_KV]).start()

            @pl.loop(1, NX * NC, unroll=True)
            def _(k):
                pages_to(lax.rem(myx + lax.div(k, NC), NX), lax.rem(myc + k, NC))
        elif len(cores) == 2:

            @pl.loop(0, NX * NC, unroll=True)
            def _(k):
                pages_to(lax.rem(myx + lax.div(k, NC), NX), lax.rem(myc + k, NC))
        else:

            @pl.loop(0, NX)
            def _(dx):
                pages_to(lax.rem(myx + dx, NX), cores[0])

    mine = lax.broadcasted_iota(jnp.int32, (REQ, NDEV), 0) == lax.div(me, NC)
    my_holders = jnp.sum(jnp.where(mine, holder.astype(F32), 0.0), axis=0, keepdims=True)
    block = lax.broadcasted_iota(jnp.int32, (NDEV, NDEV), 0)
    block_holder = (
        (block // (NC * NZ)) * (NC * NZ) + (block % NZ) * NC + (block // NZ) % NC
    ).astype(F32)
    entry = lax.broadcasted_iota(jnp.int32, (8, NDEV), 1).astype(F32)
    found_at = dot(entry, (my_holders == block_holder).astype(F32), NT)
    key = lax.broadcasted_iota(jnp.int32, (NDEV, PREFIX), 1)
    spread = (key // PAGE == lax.broadcasted_iota(jnp.int32, (NDEV, PREFIX), 0)).astype(F32)
    position = dot(found_at, spread) * PAGE + (
        lax.broadcasted_iota(jnp.int32, (8, PREFIX), 1) % PAGE
    ).astype(F32)
    length = jnp.full((8, PREFIX), prefix_len[lax.div(me, NC)]).astype(F32)
    bias[...] = jnp.where(position < length, 0.0, HIDDEN)

    to_smem.wait()
    own_maps.wait()
    spread_maps(myz)
    own_pages.wait()
    spread_pages(0, pool_own, 0)
    for step in (1, 2):
        for side in range(2):
            z = on_ring(-step * ways[side])
            wait_for(bcbuf.at[myx, myc, z], ring_bc.at[side, step - 1])
            pass_maps(step + 1, side, None)
            if step == 2:
                pass_maps(4, side, None, 2, map_rows(side))
        for part in range(PARTS):
            for side in range(2):
                wait_for(
                    held[side][step - 1].at[page_rows(part)], ring_pg.at[side, step - 1, part]
                )
                if step == 1:
                    pass_pages(2, side, part)
        for side in range(2):
            spread_maps(on_ring(-step * ways[side]))
        if step == 2:
            for side in range(2):
                spread_pages(5 + side, held[side][1], -2 * ways[side], 2 * ways[side], (side,))
            for side in range(2):
                spread_pages(7 + side, held[side][1], -2 * ways[side], ways[side])
        for side in range(2):
            spread_pages(2 * step - 1 + side, held[side][step - 1], -step * ways[side])

    for side in range(2):
        z = on_ring(-3 * ways[side])
        wait_for(bcbuf.at[myx, myc, z], ring_bc.at[side, 2])
        spread_maps(z)
    far = on_ring(4)
    for side in range(2):
        wait_for(bcbuf.at[myx, myc, far, map_rows(side)], ring_bc.at[side, 3])
    spread_maps(far)
    @pl.loop(1, NDEV)
    def _(step):
        to = peer(step)
        remote(
            dt_stage.at[to], dtbuf.at[myz, myx, myc], send.at[S_DT], recv.at[R_DT], {"dev": to}
        ).start()

    send_far()
    send_both_ways(3)

    def maps_to_other_core():
        for dx in range(NX):
            block = bcbuf.at[lax.rem(myx + NX - dx, NX), myc]
            if dx:
                wait_for(block, recv_bx.at[dx])
            remote(block, block, send.at[S_CORE], recv_c.at[dx], {"dev": other}).start()

    maps_to_other_core()
    send_both_ways(2)
    send_both_ways(1)
    wait_for(qbuf, recv.at[R_Q])
    wait_for(newbuf, recv.at[R_NK])
    wait_for(kvbuf, recv.at[R_KV])
    causal = lax.broadcasted_iota(jnp.int32, (NEW, NEW), 0) >= lax.broadcasted_iota(
        jnp.int32, (NEW, NEW), 1
    )
    for p in range(PHASES):
        @pl.loop(p * PER_PHASE * QPER, (p + 1) * PER_PHASE * QPER)
        def _(qh):
            h = lax.div(qh, QPER)
            head_cols = pl.ds(pl.multiple_of(h * 128, 128), 128)
            q = qbuf[:, pl.ds(pl.multiple_of(qh * 128, 128), 128)]
            keys = kvbuf[h, 0].reshape(PREFIX, 128)
            values = kvbuf[h, 1].reshape(PREFIX, 128)
            old = dot(q, keys, NT) + bias[0:1, :]
            new = jnp.where(causal, dot(q, newbuf[0, :, head_cols], NT), HIDDEN)
            top = jnp.maximum(
                jnp.max(old, axis=1, keepdims=True), jnp.max(new, axis=1, keepdims=True)
            )
            shift = top * EXP2_SCALE
            old = jnp.exp2(old * EXP2_SCALE - shift)
            new = jnp.exp2(new * EXP2_SCALE - shift)
            totals = jnp.sum(old, axis=1, keepdims=True) + jnp.sum(new, axis=1, keepdims=True)
            mixed = dot(old.astype(BF16), values) + dot(
                new.astype(BF16), newbuf[1, :, head_cols]
            )
            obuf[:, pl.ds(pl.multiple_of(qh * 128, 128), 128)] = (mixed / totals).astype(BF16)

        width = QHALF // PHASES
        src_cols = pl.ds(p * width, width)
        dst_cols = pl.ds(pl.multiple_of(myc * QHALF + p * width, width), width)
        pltpu.make_async_copy(
            obuf.at[my_rows, src_cols], attn_v.at[:, dst_cols], recv.at[R_OUT]
        ).start()
        remote(
            obuf.at[pl.ds(pl.multiple_of((1 - myc) * TOK, TOK), TOK), src_cols],
            attn_v.at[:, dst_cols],
            send.at[S_OUT],
            recv.at[R_OUT],
            {"dev": other},
        ).start()

    wait_for(dtbuf, recv.at[R_DT])
    wait_for(states.at[pl.ds(0, NG - 1)], recv.at[R_ST])
    for dx in range(NX):
        wait_for(bcbuf.at[lax.rem(myx + NX - dx, NX), 1 - myc], recv_c.at[dx])

    for r in range(REQ):
        for c in range(NC):
            dt_rows[2 * r : 2 * r + 2, c * TOK : (c + 1) * TOK] = dtbuf[r % NZ, r // NZ, c]
    odd_row = lax.broadcasted_iota(jnp.int32, (2 * REQ, NEW), 0) % 2 == 1
    rate = -jnp.exp(
        jnp.where(odd_row, jnp.full((2 * REQ, NEW), a_log[1]), jnp.full((2 * REQ, NEW), a_log[0]))
    )
    earlier = lax.broadcasted_iota(jnp.int32, (NEW, NEW), 0)
    later = lax.broadcasted_iota(jnp.int32, (NEW, NEW), 1)
    cumulative = dot(
        dt_rows[...] * (rate * LOG2E),
        (earlier <= later).astype(F32),
        precision=lax.Precision.HIGHEST,
    )
    less_step = cumulative - jnp.log2(dt_rows[...])
    for r in range(REQ):
        by_req[r, 0:2, :] = cumulative[2 * r : 2 * r + 2]
        by_req[r, 2:4, :] = less_step[2 * r : 2 * r + 2]

    consts = ssd_constants(d_skip)

    @pl.loop(0, NZ - 2)
    def _(i):
        j = lax.rem(i + NZ - 3, NZ - 2)
        odd = lax.rem(j, 2)
        dz = 4 + (1 - odd) * lax.div(j, 2) - odd * lax.div(j + 1, 2)
        dz = dz * lax.div(i + NZ - 1, NZ)
        rz = lax.rem(myz + NZ - dz, NZ)
        wait_for(xbuf.at[rz], recv_x.at[dz])
        for rx in range(NX):
            r = rx * NZ + rz
            rows = pl.ds(pl.multiple_of(r * NEW, NEW), NEW)
            ssd_v[rows, :], fin_v[r] = ssd_request(
                consts, by_req, xbuf, bcbuf, states, owners, rx, rz
            )

    for dz in (1, NZ - 1):
        wait_for(xbuf.at[lax.rem(myz + NZ - dz, NZ)], recv_x.at[dz])

    wait_for(attn_v, recv.at[R_OUT])
    wait_for(xbuf.at[pl.ds(0, NZ - 1)], send.at[S_X])
    wait_for(xbuf.at[0, pl.ds(0, NX - 1)], send.at[S_X])
    wait_for(xbuf.at[0, 0, 0], send.at[S_X])
    wait_for(dtbuf.at[pl.ds(0, NZ - 1)], send.at[S_DT])
    wait_for(dtbuf.at[0, pl.ds(0, NX - 1)], send.at[S_DT])
    wait_for(dtbuf.at[0, 0, 0], send.at[S_DT])
    wait_for(states.at[pl.ds(0, NG - 1)], send.at[S_ST])
    wait_for(qbuf.at[pl.ds(0, TOK)], send.at[S_Q])
    wait_for(newbuf.at[0], send.at[S_NK])
    wait_for(bcbuf.at[0, 0, pl.ds(0, NZ - 1)], send.at[S_BC])
    for pages in held[0] + held[1]:
        wait_for(pages, send.at[S_PG])
    wait_for(bcbuf.at[pl.ds(0, NX - 1), 0], send.at[S_BX])
    wait_for(bcbuf.at[:, 0], send.at[S_CORE])
    wait_for(obuf.at[pl.ds(0, TOK)], send.at[S_OUT])
    wait_for(stage.at[pl.ds(0, 7)], send.at[S_KV])
    wait_for(stage.at[0, 0], send.at[S_KV])
    wait_for(stage.at[0, 0, 0], send.at[S_KV])


def hand_over(
    owners,
    d_skip,
    ssd_v,
    fin_v,
    attn_v,
    xbuf,
    bcbuf,
    states,
    by_req,
    ssd_out,
    fin_out,
    attn_out,
    ssd_last,
    fin_last,
    sem,
):
    myz = lax.rem(lax.div(lax.axis_index("dev"), NC), NZ)

    def rows_of(r):
        return pl.ds(pl.multiple_of(r * NEW, NEW), NEW)

    def write(ssd, fin, r):
        pltpu.make_async_copy(ssd, ssd_out.at[rows_of(r)], sem.at[0]).start()
        pltpu.make_async_copy(fin, fin_out.at[r], sem.at[1]).start()

    pltpu.make_async_copy(attn_v, attn_out, sem.at[2]).start()

    @pl.loop(0, NZ - 3)
    def _(i):
        for rx in range(NX):
            r = rx * NZ + lax.rem(myz + 2 + i, NZ)
            write(ssd_v.at[rows_of(r)], fin_v.at[r], r)

    for rx in range(NX):
        r = rx * NZ + myz
        write(ssd_v.at[rows_of(r)], fin_v.at[r], r)

    consts = ssd_constants(d_skip)

    @pl.loop(0, 2)
    def _(side):
        rz = lax.rem(myz + NZ - 1 + 2 * side, NZ)
        for rx in range(NX):
            ssd_last[side, rx], fin_last[side, rx] = ssd_request(
                consts, by_req, xbuf, bcbuf, states, owners, rx, rz
            )
        for rx in range(NX):
            write(ssd_last.at[side, rx], fin_last.at[side, rx], rx * NZ + rz)

    pltpu.make_async_copy(ssd_out, ssd_out, sem.at[0]).wait()
    pltpu.make_async_copy(fin_out, fin_out, sem.at[1]).wait()
    pltpu.make_async_copy(attn_v, attn_out, sem.at[2]).wait()


def on_device(
    x_rows,
    dt_rows,
    bc_rows,
    a_log,
    d_skip,
    state_pool,
    owners,
    queries,
    new_kv,
    page_pool,
    page_table,
    prefix_len,
):
    smem = pl.BlockSpec(memory_space=pltpu.SMEM)
    vmem = pl.BlockSpec(memory_space=pltpu.VMEM)
    hbm = pl.BlockSpec(memory_space=pl.ANY)
    dma = pltpu.SemaphoreType.DMA
    left = pl.pallas_call(
        kernel,
        out_shape=(
            pltpu.VMEM((REQ * NEW, 128), BF16),
            pltpu.VMEM((REQ, 128, 128), F32),
            pltpu.VMEM((TOK, 2 * QHALF), BF16),
            pltpu.VMEM((NZ, NX, NC, TOK, 128), BF16),
            pltpu.VMEM((NX, NC, NZ, TOK, 256), BF16),
            pltpu.VMEM((NG, 16, 128, 128), BF16),
            pltpu.VMEM((REQ, 8, NEW), F32),
        ),
        in_specs=[smem] * 4 + [vmem, vmem, hbm, hbm, vmem, hbm, hbm, hbm],
        out_specs=(vmem,) * 7,
        scratch_shapes=[
            pltpu.VMEM((NZ, NX, NC, 2, TOK), F32),
            *[pltpu.VMEM((HELD, PAGE, 4 * HALF), BF16)] * 5,
            pltpu.VMEM((ROUTES, NX, NC, HEADS_CORE, 2, PAGE, 128), BF16),
            pltpu.VMEM((HEADS_CORE, 2, NX, NC, NZ, PAGE, 128), BF16),
            pltpu.VMEM((NEW, QHALF), BF16),
            pltpu.VMEM((2, NEW, HALF), BF16),
            pltpu.VMEM((NEW, QHALF), BF16),
            pltpu.VMEM((2 * REQ, NEW), F32),
            pltpu.VMEM((NDEV, 2, TOK), F32),
            pltpu.VMEM((REQ, 128), jnp.int32),
            pltpu.SMEM((REQ, 128), jnp.int32),
            pltpu.VMEM((8, PREFIX), F32),
            dma((8,)),
            dma((11,)),
            dma((2, 4)),
            dma((2, 2, PARTS)),
            dma((NZ,)),
            dma((NX,)),
            dma((NX,)),
            dma((1,)),
        ],
        compiler_params=pltpu.CompilerParams(
            collective_id=0, has_side_effects=True, vmem_limit_bytes=46 * 1024 * 1024
        ),
    )(
        owners,
        a_log,
        d_skip,
        prefix_len,
        page_table,
        dt_rows,
        x_rows,
        bc_rows,
        state_pool.reshape(16, 128, 128),
        queries,
        new_kv,
        page_pool,
    )
    ssd_out, finals, attn_out = pl.pallas_call(
        hand_over,
        out_shape=tuple(jax.ShapeDtypeStruct(a.shape, a.dtype) for a in left[:3]),
        in_specs=[smem] * 2 + [vmem] * 7,
        out_specs=(hbm,) * 3,
        scratch_shapes=[
            pltpu.VMEM((2, NX, NEW, 128), BF16),
            pltpu.VMEM((2, NX, 128, 128), F32),
            dma((3,)),
        ],
        compiler_params=pltpu.CompilerParams(vmem_limit_bytes=16 * 1024 * 1024),
    )(owners, d_skip, *left)
    return ssd_out, finals.reshape(REQ, 2, 64, 128), attn_out


def solution(mesh):
    return jax.shard_map(
        on_device,
        mesh=mesh,
        in_specs=(
            P(("grp", "dev"), None),
            P(("grp", "dev"), None),
            P(("grp", "dev"), None),
            P("dev"),
            P("dev"),
            P("grp", "dev", None, None),
            P("grp"),
            P(("grp", "dev"), None),
            P(("grp", "dev"), None),
            P(("grp", "dev"), None, None),
            P("grp", None),
            P("grp"),
        ),
        out_specs=(P("grp", "dev"), P("grp", "dev", None, None), P(("grp", "dev"), None)),
        check_vma=False,
    )
```
